256 devices in a mesh: grp: 8 (over z_lo, core), resp: 32 (over x, y, z_hi).
Axes of the slice: x: 4, y: 4, z: 8 (z_hi: 2, z_lo: 4; z = z_hi * 4 + z_lo), core: 2. Of those that a mesh axis runs over, the one named last changes fastest.
Arguments:
- hidden: bfloat16 [32768, 5120], P(('grp', 'resp')), may hold values from -6 to 6
- queries: bfloat16 [32768, 4096], P(('grp', 'resp')), may hold values from -6 to 6
- answer_token_keys: bfloat16 [32768, 512], P(('grp', 'resp')), may hold values from -6 to 6
- answer_token_values: bfloat16 [32768, 512], P(('grp', 'resp')), may hold values from -6 to 6
- cotangent: bfloat16 [32768, 4096], P(('grp', 'resp')), may hold values from -6 to 6
- slot_answer_index: int32 [32768], P(('grp', 'resp')), may hold values from -1 to 63, as said below
- rewards: float32 [8, 64], P('grp'), may hold values from -4 to 4
- group_prompt_keys: bfloat16 [16384, 512], P(('grp', 'resp')), may hold values from -6 to 6
- group_prompt_values: bfloat16 [16384, 512], P(('grp', 'resp')), may hold values from -6 to 6
- adapter_down_matrix: bfloat16 [5120, 64], replicated, may hold values from -0.078125 to 0.078125
- adapter_up_matrix: bfloat16 [64, 4096], replicated, may hold values from -0.75 to 0.75
Outputs:
- prompt_dk: bfloat16 [16384, 512], P(('grp', 'resp'))
- prompt_dv: bfloat16 [16384, 512], P(('grp', 'resp'))
- resp_dk: bfloat16 [32768, 512], P(('grp', 'resp'))
- resp_dv: bfloat16 [32768, 512], P(('grp', 'resp'))
- grad_a: float32 [5120, 64], replicated
- up_matrix_gradient: float32 [64, 4096], replicated
The draws below stay inside these ranges and needn't reach their ends.
Inputs may be any that keep to these rules, and one draw needn't show every extreme that they name: `slot_answer_index`: the 128 slots of the device of index r along resp hold responses 2 r and 2 r + 1 of its group, in that order in consecutive slots, each 1 to 64 long, then empty slots.
All inputs are finite; a program needn't handle non-finite values.
Results may differ from the reference program's by a relative error of at most 0.013.
The reference program's roundings to bfloat16 on the way count: a program that leaves them out, or rounds other values in their place, can miss the bound.
Values may be sent and summed in bfloat16 or wider, within the bound.
A program may use at most 192 MiB of HBM per device.

```python
import jax
import jax.numpy as jnp
from jax import lax

MODEL_WIDTH = 5120
HEADS = 32
KV_HEADS = 4
HEAD_DIM = 128
ADAPTER_RANK = 64
CAP = 128
GROUPS = 8
RESP_N = 64
PROMPT = 2048
ROWS = 32768
KVD = 512
QUERY_FEATURES = 4096
N_RESP = 32


def draw_slot_answer_index(key, part):
    key = jax.random.fold_in(key, 11)
    device_count = GROUPS * N_RESP
    drawn_len = jax.random.randint(key, (device_count, 2), CAP // 8, CAP // 2 + 1)
    local_rank = jnp.arange(device_count, dtype=jnp.int32) % N_RESP
    lengths = jnp.where((local_rank == 0)[:, None], CAP // 2, drawn_len)
    lengths = jnp.where((local_rank == 1)[:, None], CAP // 8, lengths)
    positions = jnp.arange(CAP, dtype=jnp.int32)[None, :]
    first_len = lengths[:, :1]
    pair_len = first_len + lengths[:, 1:]
    which_one = jnp.where(positions < first_len, 0, jnp.where(positions < pair_len, 1, -1))
    resp_index = jnp.where(which_one >= 0, 2 * local_rank[:, None] + which_one, -1)
    return resp_index.reshape(-1).astype(jnp.int32)


def draw_group_prompt_keys(key, part):
    key = jax.random.fold_in(key, 21)
    row_total = GROUPS * PROMPT
    return jax.random.truncated_normal(key, -6.0, 6.0, (row_total, KVD), jnp.float32).astype(jnp.bfloat16)


def draw_queries(key, part):
    key = jax.random.fold_in(key, 22)
    return jax.random.truncated_normal(key, -6.0, 6.0, (ROWS, QUERY_FEATURES), jnp.float32).astype(jnp.bfloat16)


def block_scale(stream_key, dims, pieces, least, top_value):
    loudness = 1.0
    for dim, parts in pieces:
        draws = jax.random.uniform(jax.random.fold_in(jax.random.fold_in(stream_key, 6), dim), (parts,), jnp.float32, least / len(pieces), top_value / len(pieces))
        loudness = loudness * jnp.repeat(jnp.exp(draws), dims[dim] // parts).reshape((-1,) + (1,) * (len(dims) - 1 - dim))
    return loudness


def gaussian(rng, dims, scale, reach, shards=(), kind=jnp.bfloat16):
    array = scale * jax.random.normal(rng, dims, jnp.float32)
    if shards:
        array = array * block_scale(rng, dims, shards, -0.22, 0.18)
    return jnp.clip(array, -reach, reach).astype(kind)


def setup_inputs(seed: int = 0) -> dict:
    keys = jax.random.split(jax.random.key(seed), 12)
    return {
        "hidden": gaussian(keys[0], (ROWS, MODEL_WIDTH), 1.0, 6.0, ((0, 256),)),
        "queries": draw_queries(jax.random.fold_in(keys[11], 71), 0),
        "answer_token_keys": gaussian(keys[2], (ROWS, KVD), 1.0, 6.0, ((0, 256),)),
        "answer_token_values": gaussian(keys[3], (ROWS, KVD), 1.0, 6.0, ((0, 256),)),
        "cotangent": gaussian(keys[4], (ROWS, QUERY_FEATURES), 1.0, 6.0, ((0, 256),)),
        "slot_answer_index": draw_slot_answer_index(jax.random.fold_in(keys[11], 71), 0),
        "rewards": gaussian(keys[6], (GROUPS, RESP_N), 1.0, 4.0, ((0, 8),), jnp.float32),
        "group_prompt_keys": draw_group_prompt_keys(jax.random.fold_in(keys[11], 71), 0),
        "group_prompt_values": gaussian(keys[8], (GROUPS * PROMPT, KVD), 1.0, 6.0, ((0, 256),)),
        "adapter_down_matrix": gaussian(keys[9], (MODEL_WIDTH, ADAPTER_RANK), MODEL_WIDTH ** -0.5, 0.078125),
        "adapter_up_matrix": gaussian(keys[10], (ADAPTER_RANK, QUERY_FEATURES), ADAPTER_RANK ** -0.5, 0.75),
    }


ADAPTER_SCALE = 2.0

def attend_back(query_h, grad_out, all_keys, all_values, visible):
    factor = query_h.shape[-1] ** (-0.5)
    scores = jnp.einsum('gch,kh->gck', query_h.astype(jnp.float32), all_keys.astype(jnp.float32)) * factor
    scores = jnp.where(visible[None], scores, -1e+30)
    row_max = lax.optimization_barrier(jnp.max(scores, axis=-1, keepdims=True))
    unnorm = jnp.exp(scores - row_max)
    probs = unnorm / lax.optimization_barrier(jnp.sum(unnorm, axis=-1, keepdims=True))
    probs_bf = probs.astype(jnp.bfloat16)
    attended = jnp.einsum('gck,kh->gch', probs_bf.astype(jnp.float32), all_values.astype(jnp.float32))
    grad_prob = jnp.einsum('gch,kh->gck', grad_out.astype(jnp.float32), all_values.astype(jnp.float32))
    delta_row = lax.optimization_barrier(jnp.sum(grad_out.astype(jnp.float32) * attended, axis=-1, keepdims=True))
    grad_score = (probs * (grad_prob - delta_row) * factor).astype(jnp.bfloat16)
    grad_query = jnp.einsum('gck,kh->gch', grad_score.astype(jnp.float32), all_keys.astype(jnp.float32))
    grad_key = jnp.einsum('gck,gch->kh', grad_score.astype(jnp.float32), query_h.astype(jnp.float32))
    grad_value = jnp.einsum('gck,gch->kh', probs_bf.astype(jnp.float32), grad_out.astype(jnp.float32))
    return (grad_query, grad_key, grad_value)

def slot_weights(answer_slots, reward_entries_row):
    average = jnp.mean(reward_entries_row)
    spread = jnp.mean((reward_entries_row - average) * (reward_entries_row - average))
    advantage = (reward_entries_row - average) / jnp.sqrt(spread + 1e-05)
    resp_ids = jnp.arange(reward_entries_row.shape[0], dtype=jnp.int32)
    onehot = (answer_slots[:, None] == resp_ids[None, :]).astype(jnp.float32)
    counts = lax.optimization_barrier(jnp.sum(onehot, axis=0))
    return lax.optimization_barrier(jnp.sum(onehot * (advantage / jnp.maximum(counts, 1.0))[None, :], axis=1))

def visibility(answer_slots, prompt_len):
    row_count = answer_slots.shape[0]
    positions = jnp.arange(row_count, dtype=jnp.int32)
    same_resp = (answer_slots[:, None] == answer_slots[None, :]) & (answer_slots[:, None] >= 0) & (positions[None, :] <= positions[:, None])
    return jnp.concatenate([jnp.ones((row_count, prompt_len), dtype=bool), same_resp], axis=1)

def attention_block_backward(hidden, queries, answer_token_keys, answer_token_values, cotangent, answer_slots, prompt_key_rows, prompt_value_rows, reward_entries_row, adapter_down_matrix, adapter_up_matrix):
    row_count = queries.shape[0]
    prompt_len = prompt_key_rows.shape[0]
    weights = slot_weights(answer_slots, reward_entries_row)
    grad_all = (cotangent.astype(jnp.float32) * weights[:, None]).astype(jnp.bfloat16)
    visible = visibility(answer_slots, prompt_len)
    group_heads = HEADS // KV_HEADS
    span = group_heads * HEAD_DIM
    query_parts, key_pre, value_pre, key_resp, value_resp = ([], [], [], [], [])
    for kv_index in range(KV_HEADS):
        query_h = queries[:, kv_index * span:(kv_index + 1) * span].reshape(row_count, group_heads, HEAD_DIM).transpose(1, 0, 2)
        grad_out = grad_all[:, kv_index * span:(kv_index + 1) * span].reshape(row_count, group_heads, HEAD_DIM).transpose(1, 0, 2)
        low_col = kv_index * HEAD_DIM
        high_col = low_col + HEAD_DIM
        all_keys = jnp.concatenate([prompt_key_rows[:, low_col:high_col], answer_token_keys[:, low_col:high_col]], axis=0)
        all_values = jnp.concatenate([prompt_value_rows[:, low_col:high_col], answer_token_values[:, low_col:high_col]], axis=0)
        grad_query, grad_key, grad_value = attend_back(query_h, grad_out, all_keys, all_values, visible)
        query_parts.append(grad_query.transpose(1, 0, 2).reshape(row_count, span))
        key_pre.append(grad_key[:prompt_len])
        value_pre.append(grad_value[:prompt_len])
        key_resp.append(grad_key[prompt_len:])
        value_resp.append(grad_value[prompt_len:])
    query_rows_gradient = jnp.concatenate(query_parts, axis=1).astype(jnp.bfloat16)
    reduced_projection = jnp.dot(hidden, adapter_down_matrix, preferred_element_type=jnp.float32).astype(jnp.bfloat16)
    up_matrix_gradient = ADAPTER_SCALE * jnp.dot(reduced_projection.T, query_rows_gradient, preferred_element_type=jnp.float32)
    backward_reduced = (ADAPTER_SCALE * jnp.dot(query_rows_gradient, adapter_up_matrix.T, preferred_element_type=jnp.float32)).astype(jnp.bfloat16)
    grad_a = jnp.dot(hidden.T, backward_reduced, preferred_element_type=jnp.float32)
    return (jnp.concatenate(key_resp, axis=1).astype(jnp.bfloat16), jnp.concatenate(value_resp, axis=1).astype(jnp.bfloat16), jnp.concatenate(key_pre, axis=1), jnp.concatenate(value_pre, axis=1), grad_a, up_matrix_gradient)

def reference(hidden, queries, answer_token_keys, answer_token_values, cotangent, slot_answer_index, rewards, group_prompt_keys, group_prompt_values, adapter_down_matrix, adapter_up_matrix):
    per_group = N_RESP * CAP
    grad_a = jnp.zeros((MODEL_WIDTH, ADAPTER_RANK), jnp.float32)
    up_matrix_gradient = jnp.zeros((ADAPTER_RANK, QUERY_FEATURES), jnp.float32)
    prompt_k_out, prompt_v_out, resp_k_out, resp_v_out = ([], [], [], [])
    for group in range(GROUPS):
        prompt_key_rows = group_prompt_keys[group * PROMPT:(group + 1) * PROMPT]
        prompt_value_rows = group_prompt_values[group * PROMPT:(group + 1) * PROMPT]
        reward_entries_row = rewards[group]
        blocks = tuple((arr[group * per_group:(group + 1) * per_group].reshape((N_RESP, CAP) + arr.shape[1:]) for arr in (hidden, queries, answer_token_keys, answer_token_values, cotangent, slot_answer_index)))

        def scan_step(running, attention_block):
            key_acc, value_acc, acc_a, acc_b = running
            answer_key_slice, answer_value_slice, prompt_key_slice, prompt_value_slice, first_portion, second_portion = attention_block_backward(*attention_block, prompt_key_rows, prompt_value_rows, reward_entries_row, adapter_down_matrix, adapter_up_matrix)
            return ((key_acc + prompt_key_slice, value_acc + prompt_value_slice, acc_a + first_portion, acc_b + second_portion), (answer_key_slice, answer_value_slice))
        initial = (jnp.zeros((PROMPT, KVD), jnp.float32), jnp.zeros((PROMPT, KVD), jnp.float32), grad_a, up_matrix_gradient)
        running, stacked = lax.scan(scan_step, initial, blocks)
        key_acc, value_acc, grad_a, up_matrix_gradient = running
        prompt_k_out.append(key_acc.astype(jnp.bfloat16))
        prompt_v_out.append(value_acc.astype(jnp.bfloat16))
        resp_k_out.append(stacked[0].reshape(per_group, KVD))
        resp_v_out.append(stacked[1].reshape(per_group, KVD))
    return (jnp.concatenate(prompt_k_out, axis=0), jnp.concatenate(prompt_v_out, axis=0), jnp.concatenate(resp_k_out, axis=0), jnp.concatenate(resp_v_out, axis=0), grad_a, up_matrix_gradient)
```

```python
import jax
import jax.numpy as jnp
from jax import lax
from jax.experimental import pallas as pl
from jax.experimental.pallas import tpu as pltpu
from jax.sharding import PartitionSpec as P

BF = jnp.bfloat16
F32 = jnp.float32
SLOTS = 128
D = 128
KVH = 4
QH = 8
SPAN = QH * D
PROMPT = 2048
RANK = 64
WIDTH = 5120
FEATURES = 4096
AW = WIDTH // KVH // 2
UW = SPAN // 2
PW = AW + UW
FACTOR = D**-0.5
LOG2E_FACTOR = FACTOR * 1.4426950408889634
NN = (((1,), (0,)), ((), ()))
NT = (((1,), (1,)), ((), ()))


def mm(a, b, dims=NN):
    return lax.dot_general(a, b, dims, preferred_element_type=F32)


def fold(x, op):
    rows, lanes = x.shape
    return op(x.reshape(rows // 8, 8, lanes), axis=0)


def lanes(start, size):
    return pl.ds(pl.multiple_of(start, 128), size)


def kernel(
    hidden, queries, ans_k, ans_v, cot, slots, rewards, prompt_k, prompt_v, down, up,
    pdk_out, pdv_out, rdk_out, rdv_out, ff_out,
    zb, kv, qb, gb, rkv, small, gfull,
    s_ref, dp_ref, ds_ref, kt, dkv, bl_send, bl, rd_send, rd, up_acc, blt,
    sb, yb, zs, zr, pf, pr, ysum,
    a_own, a_send, a_recv, u_own, u_send, u_recv, x_send, x_recv, y_send, y_recv, z_all, ff,
    send_sem, recv_sem, blk_send, blk_recv, out_send, out_recv,
):
    g = lax.axis_index("grp")
    r = lax.axis_index("resp")
    zl, core = lax.div(g, 2), lax.rem(g, 2)
    x, y, z = lax.div(r, 8), lax.rem(lax.div(r, 2), 4), lax.rem(r, 2)

    def at(gg, xx, yy, zz):
        return (gg, xx * 8 + yy * 2 + zz)

    xs = [lax.rem(x + d, 4) for d in range(4)]
    xf = [lax.rem(x + 4 - d, 4) for d in range(4)]
    ys = [lax.rem(y + d, 4) for d in range(4)]
    yf = [lax.rem(y + 4 - d, 4) for d in range(4)]
    x_dev = [at(g, xs[d], y, z) for d in range(4)]
    y_dev = [at(g, x, ys[d], z) for d in range(4)]
    z_dev = at(g, x, y, 1 - z)
    c_dev = at(zl * 2 + 1 - core, x, y, z)
    ring = []
    for dz in range(4):
        for e in range(2):
            if dz or e:
                zz = z if e == 0 else 1 - z
                ring.append((dz, e, lax.rem(zl + dz, 4), lax.rem(zl + 4 - dz, 4), zz))

    barrier = pltpu.get_barrier_semaphore()
    peers = x_dev[1:] + y_dev[1:] + [c_dev]
    peers += [at(to * 2 + core, x, y, zz) for dz, e, to, frm, zz in ring]
    for peer in peers:
        pl.semaphore_signal(barrier, inc=1, device_id=peer, device_id_type=pl.DeviceIdType.MESH)
    pl.semaphore_wait(barrier, len(peers))

    sent = []
    names = {}

    def sem(name):
        return names.setdefault(name, len(names))

    def copy(name, src, dst, dev):
        k = sem(name)
        return pltpu.make_async_remote_copy(
            src_ref=src, dst_ref=dst, send_sem=send_sem.at[k], recv_sem=recv_sem.at[k],
            device_id=dev, device_id_type=pl.DeviceIdType.MESH,
        )

    def send(name, src, dst, dev):
        c = copy(name, src, dst, dev)
        c.start()
        sent.append(c)

    def recv(name, dst, dev):
        copy(name, dst, dst, dev).wait_recv()

    def half(zz):
        return pl.ds(pl.multiple_of(zz * 64, 64), 64)

    send("z0", prompt_k, zb.at[0], z_dev)
    send("z1", prompt_v, zb.at[1], z_dev)
    for d in (1, 3, 2):
        send(("xa0", d), prompt_k.at[:, lanes(xs[d] * D, D)], kv.at[0, x, y, half(z)], x_dev[d])
        send(("xa1", d), prompt_v.at[:, lanes(xs[d] * D, D)], kv.at[1, x, y, half(z)], x_dev[d])
    kv[0, x, y, half(z), :] = prompt_k[:, lanes(x * D, D)]
    kv[1, x, y, half(z), :] = prompt_v[:, lanes(x * D, D)]

    across = jnp.broadcast_to(slots[...].astype(F32), (SLOTS, SLOTS))
    down_rows = across.T
    first = lax.broadcasted_iota(jnp.int32, (SLOTS, SLOTS), 0)
    second = lax.broadcasted_iota(jnp.int32, (SLOTS, SLOTS), 1)
    same = across == down_rows
    seen = same & (down_rows >= 0.0) & (first <= second)
    small[x, 0:SLOTS, :] = jnp.where(seen, 1.0, 0.0).astype(BF)
    reward = rewards[...]
    centred = reward - jnp.mean(reward, axis=1, keepdims=True)
    advantage = centred / jnp.sqrt(jnp.mean(centred * centred, axis=1, keepdims=True) + 1e-5)
    counts = jnp.sum(jnp.where(same, 1.0, 0.0), axis=1, keepdims=True)
    holds = down_rows[:, :64] == second[:, :64].astype(F32)
    weight = jnp.sum(jnp.where(holds, advantage, 0.0), axis=1, keepdims=True)
    weight = weight / jnp.maximum(counts, 1.0)
    for c in range(0, FEATURES, 512):
        gfull[:, c : c + 512] = (cot[:, c : c + 512].astype(F32) * weight).astype(BF)

    for d in (1, 2, 3):
        recv(("xa0", d), kv.at[0, xf[d], y, half(z)], x_dev[d])
        recv(("xa1", d), kv.at[1, xf[d], y, half(z)], x_dev[d])
    for d in (1, 2, 3):
        send(("ya", d), kv.at[:, :, y, half(z)], kv.at[:, :, y, half(z)], y_dev[d])

    low = mm(hidden[...], down[...])
    small[x, SLOTS : SLOTS + RANK, :] = low.T.astype(BF)

    recv("z0", zb.at[0], z_dev)
    recv("z1", zb.at[1], z_dev)
    for d in (1, 3, 2):
        for n in range(2):
            send(
                ("xb", n, d), zb.at[n, :, lanes(xs[d] * D, D)],
                kv.at[n, x, y, half(1 - z)], x_dev[d],
            )
    for n in range(2):
        kv[n, x, y, half(1 - z), :] = zb[n, :, lanes(x * D, D)]

    def block_copies(i, src, dev, to):
        pairs = (
            (queries.at[:, lanes(to * SPAN, SPAN)], qb.at[src]),
            (gfull.at[:, lanes(to * SPAN, SPAN)], gb.at[src]),
            (ans_k.at[:, lanes(to * D, D)], rkv.at[src, 0]),
            (ans_v.at[:, lanes(to * D, D)], rkv.at[src, 1]),
            (small.at[x], small.at[src]),
        )
        return [
            pltpu.make_async_remote_copy(
                src_ref=a, dst_ref=b, send_sem=blk_send.at[n, i], recv_sem=blk_recv.at[n, i],
                device_id=dev, device_id_type=pl.DeviceIdType.MESH,
            )
            for n, (a, b) in enumerate(pairs)
        ]

    for i, d in ((1, 1), (2, 3), (3, 2)):
        for c in block_copies(i, x, x_dev[d], xs[d]):
            c.start()
            sent.append(c)

    for d in (1, 2, 3):
        for n in range(2):
            recv(("xb", n, d), kv.at[n, xf[d], y, half(1 - z)], x_dev[d])
    for d in (1, 2, 3):
        send(("yb", d), kv.at[:, :, y, half(1 - z)], kv.at[:, :, y, half(1 - z)], y_dev[d])

    qb[x] = queries[:, lanes(x * SPAN, SPAN)]
    gb[x] = gfull[:, lanes(x * SPAN, SPAN)]
    rkv[x, 0] = ans_k[:, lanes(x * D, D)]
    rkv[x, 1] = ans_v[:, lanes(x * D, D)]
    dkv[...] = jnp.zeros_like(dkv)
    up_acc[...] = jnp.zeros_like(up_acc)
    for d in (1, 2, 3):
        recv(("ya", d), kv.at[:, :, yf[d], half(z)], y_dev[d])
    for d in (1, 2, 3):
        recv(("yb", d), kv.at[:, :, yf[d], half(1 - z)], y_dev[d])
    for c in range(16):
        kt[:, c * D : (c + 1) * D] = kv[0, c // 4, c % 4].T

    def out_copies(i, src, dev):
        pairs = ((bl_send.at[i], bl.at[src]), (rd_send.at[i], rd.at[src]))
        return [
            pltpu.make_async_remote_copy(
                src_ref=a, dst_ref=b, send_sem=out_send.at[n, i], recv_sem=out_recv.at[n, i],
                device_id=dev, device_id_type=pl.DeviceIdType.MESH,
            )
            for n, (a, b) in enumerate(pairs)
        ]

    def block(i, carry):
        step = lax.rem(lax.div(i * (i + 1), 2), 4)
        src = lax.rem(x + 4 - step, 4)

        @pl.when(i > 0)
        def _():
            for c in block_copies(i, src, at(g, src, y, z), x):
                c.wait_recv()

        kt[:, PROMPT:] = rkv[src, 0].T
        mask = small[src, 0:SLOTS, :]
        mask = jnp.concatenate([mask] * QH, axis=1) > 0
        q = jnp.concatenate([qb[src, :, j * D : (j + 1) * D] for j in range(QH)], axis=0)
        go = jnp.concatenate([gb[src, :, j * D : (j + 1) * D] for j in range(QH)], axis=0)

        def rows(n, c):
            return rkv[src, n] if c == 16 else kv[n, c // 4, c % 4]

        def span(c):
            return slice(c * D, (c + 1) * D)

        top = None
        for c in range(17):
            s = mm(rows(0, c), q, NT)
            if c == 16:
                s = jnp.where(mask, s, -1e30)
            s_ref[span(c), :] = s
            part = fold(s, jnp.max)
            top = part if top is None else jnp.maximum(top, part)
        top = jnp.max(top, axis=0, keepdims=True) * LOG2E_FACTOR
        total = None
        for c in range(17):
            e = jnp.exp2(s_ref[span(c), :] * LOG2E_FACTOR - top)
            s_ref[span(c), :] = e
            part = fold(e, jnp.sum)
            total = part if total is None else total + part
        inv = 1.0 / jnp.sum(total, axis=0, keepdims=True)
        delta = None
        for c in range(17):
            dp = mm(rows(1, c), go, NT)
            pb = (s_ref[span(c), :] * inv).astype(BF)
            dp_ref[span(c), :] = dp
            part = fold(pb.astype(F32) * dp, jnp.sum)
            delta = part if delta is None else delta + part
            gv = mm(pb, go)
            if c == 16:
                rd_send[i, 1] = gv.astype(BF)
            else:
                dkv[1, c // 4, c % 4] += gv
        delta = jnp.sum(delta, axis=0, keepdims=True)
        inv = inv * FACTOR
        for c in range(17):
            ds = (s_ref[span(c), :] * inv * (dp_ref[span(c), :] - delta)).astype(BF)
            ds_ref[span(c), :] = ds
            gk = mm(ds, q)
            if c == 16:
                rd_send[i, 0] = gk.astype(BF)
            else:
                dkv[0, c // 4, c % 4] += gk
        dq = mm(kt[...], ds_ref[...]).astype(BF)
        low_t = small[src, SLOTS : SLOTS + RANK, :]
        back = jnp.zeros((RANK, SLOTS), F32)
        for j in range(QH):
            dqj = dq[:, j * D : (j + 1) * D]
            back += mm(up[:, lanes(x * SPAN + j * D, D)], dqj)
            up_acc[:, j * D : (j + 1) * D] += mm(low_t, dqj, NT)
        bl_send[i] = back

        @pl.when(i > 0)
        def _():
            for c in out_copies(i, x, at(g, src, y, z)):
                c.start()

        return carry

    lax.fori_loop(0, 4, block, 0)
    bl[x] = bl_send[0]
    rd[x] = rd_send[0]

    sb[...] = dkv[...].astype(BF)
    for d in (1, 3, 2):
        send(("gy", d), sb.at[:, :, ys[d]], yb.at[d - 1], y_dev[d])

    for i, d in ((1, 1), (2, 3), (3, 2)):
        for c in out_copies(i, xs[d], x_dev[d]):
            c.wait_recv()
    back = 2.0 * (bl[0] + bl[1] + bl[2] + bl[3])
    blt[...] = back.astype(BF)
    mine = pl.ds(pl.multiple_of(core * 32, 32), 32)
    other = pl.ds(pl.multiple_of(32 - core * 32, 32), 32)
    bl_mine, bl_other = blt[mine, :], blt[other, :]
    for n in range(2):
        piece = up_acc[other, n * UW : (n + 1) * UW].astype(BF)
        u_send[n] = piece[0:16]
        u_send[2 + n] = piece[16:32]
    for xx in range(4):
        for n in range(2):
            cols = slice((2 * xx + n) * AW, (2 * xx + n + 1) * AW)
            piece = mm(bl_other, hidden[:, cols]).astype(BF)
            a_send[xx, n] = piece[0:16]
            a_send[xx, 2 + n] = piece[16:32]
    send("ca", a_send, a_recv, c_dev)
    send("cu", u_send, u_recv, c_dev)
    for n in range(2):
        piece = up_acc[mine, n * UW : (n + 1) * UW]
        u_own[n] = piece[0:16]
        u_own[2 + n] = piece[16:32]
    for xx in range(4):
        for n in range(2):
            cols = slice((2 * xx + n) * AW, (2 * xx + n + 1) * AW)
            piece = mm(bl_mine, hidden[:, cols])
            a_own[xx, n] = piece[0:16]
            a_own[xx, 2 + n] = piece[16:32]
    recv("ca", a_recv, c_dev)
    for xx in range(4):
        part = a_own[xx] + a_recv[xx].astype(F32)
        a_own[xx] = part
        x_send[xx] = part.astype(BF)
    for d in (1, 3, 2):
        send(("rx", d), x_send.at[xs[d]], x_recv.at[d - 1], x_dev[d])
    recv("cu", u_recv, c_dev)
    u_sum = u_own[...] + u_recv[...].astype(F32)

    for d in (1, 2, 3):
        recv(("gy", d), yb.at[d - 1], y_dev[d])
    for n in range(2):
        for xx in range(4):
            part = dkv[n, xx, y]
            for d in range(3):
                part += yb[d, n, xx].astype(F32)
            ysum[n, xx] = part
            sb[n, xx, y] = part.astype(BF)
    send("gz", sb.at[:, :, y, half(1 - z)], zr, z_dev)

    for d in (1, 2, 3):
        recv(("rx", d), x_recv.at[d - 1], x_dev[d])
    a_sum = a_own[x]
    for d in range(3):
        a_sum += x_recv[d].astype(F32)
    y_send[:, :, 0:AW] = a_sum.astype(BF)
    y_send[:, :, AW:PW] = (2.0 * u_sum).astype(BF)
    ysum_a = a_sum
    a_own[x] = ysum_a
    u_own[...] = 2.0 * u_sum
    for d in (1, 3, 2):
        send(("ry", d), y_send.at[ys[d]], y_recv.at[d - 1], y_dev[d])
    for d in (1, 2, 3):
        recv(("ry", d), y_recv.at[d - 1], y_dev[d])
    part_a = a_own[x, y]
    part_u = u_own[y]
    for d in range(3):
        part_a += y_recv[d, :, 0:AW].astype(F32)
        part_u += y_recv[d, :, AW:PW].astype(F32)
    here = zl * 2 + z
    z_all[here, :, 0:AW] = part_a.astype(BF)
    z_all[here, :, AW:PW] = part_u.astype(BF)
    for dz, e, to, frm, zz in ring:
        send(("rz", dz, e), z_all.at[here], z_all.at[here], at(to * 2 + core, x, y, zz))

    recv("gz", zr, z_dev)
    for n in range(2):
        for xx in range(4):
            part = ysum[n, xx, half(z), :] + zr[n, xx].astype(F32)
            pf[xx, n] = part.astype(BF)
    for d in (1, 3, 2):
        send(("gx", d), pf.at[xs[d]], pr.at[x], x_dev[d])
    pr[x] = pf[x]

    for dz, e, to, frm, zz in ring:
        recv(("rz", dz, e), z_all.at[frm * 2 + zz], at(to * 2 + core, x, y, zz))
    total = z_all[0].astype(F32)
    for n in range(1, 8):
        total += z_all[n].astype(F32)
    ff[core, x, y] = total.astype(BF)
    for d in (1, 3, 2):
        send(("fy", d), ff.at[core, x, y], ff.at[core, x, y], y_dev[d])
    for h in range(4):
        rdk_out[:, h * D : (h + 1) * D] = rd[h, 0]
        rdv_out[:, h * D : (h + 1) * D] = rd[h, 1]
    for d in (1, 2, 3):
        recv(("gx", d), pr.at[xf[d]], x_dev[d])
    for h in range(4):
        pdk_out[:, h * D : (h + 1) * D] = pr[h, 0]
        pdv_out[:, h * D : (h + 1) * D] = pr[h, 1]
    for d in (1, 2, 3):
        recv(("fy", d), ff.at[core, x, yf[d]], y_dev[d])
    for d in (1, 3, 2):
        send(("fx", d), ff.at[core, x], ff.at[core, x], x_dev[d])
    send(("fc", 0), ff.at[core, x], ff.at[core, x], c_dev)
    for d in (1, 3, 2):
        recv(("fx", d), ff.at[core, xf[d]], x_dev[d])
        send(("fc", d), ff.at[core, xf[d]], ff.at[core, xf[d]], c_dev)
    for d in range(4):
        recv(("fc", d), ff.at[1 - core, xf[d]], c_dev)
    ff_out[...] = ff[...]

    for c in sent:
        c.wait_send()
    for i, d in ((1, 1), (2, 3), (3, 2)):
        for c in out_copies(i, x, x_dev[0]):
            c.wait_send()


def body(
    hidden, queries, answer_token_keys, answer_token_values, cotangent, slot_answer_index,
    rewards, group_prompt_keys, group_prompt_values, adapter_down_matrix, adapter_up_matrix,
):
    vmem = pl.BlockSpec(memory_space=pltpu.VMEM)
    v = pltpu.VMEM
    scratch = [
        v((2, 64, 512), BF), v((2, 4, 4, 128, D), BF),
        v((4, SLOTS, SPAN), BF), v((4, SLOTS, SPAN), BF), v((4, 2, SLOTS, D), BF),
        v((4, SLOTS + RANK, 128), BF), v((SLOTS, FEATURES), BF),
        v((PROMPT + SLOTS, SPAN), F32), v((PROMPT + SLOTS, SPAN), F32),
        v((PROMPT + SLOTS, SPAN), BF), v((D, PROMPT + SLOTS), BF),
        v((2, 4, 4, 128, D), F32),
        v((4, RANK, SLOTS), F32), v((4, RANK, SLOTS), F32),
        v((4, 2, SLOTS, D), BF), v((4, 2, SLOTS, D), BF),
        v((RANK, SPAN), F32), v((RANK, SLOTS), BF),
        v((2, 4, 4, 128, D), BF), v((3, 2, 4, 128, D), BF), v((16, 128), BF),
        v((2, 4, 64, D), BF), v((4, 2, 64, D), BF), v((4, 2, 64, D), BF),
        v((2, 4, 128, D), F32),
        v((4, 4, 16, AW), F32), v((4, 4, 16, AW), BF), v((4, 4, 16, AW), BF),
        v((4, 16, UW), F32), v((4, 16, UW), BF), v((4, 16, UW), BF),
        v((4, 4, 16, AW), BF), v((3, 4, 16, AW), BF),
        v((4, 16, PW), BF), v((3, 16, PW), BF), v((8, 16, PW), BF),
        v((2, 4, 4, 16, PW), BF),
        pltpu.SemaphoreType.DMA((64,)), pltpu.SemaphoreType.DMA((64,)),
        pltpu.SemaphoreType.DMA((5, 4)), pltpu.SemaphoreType.DMA((5, 4)),
        pltpu.SemaphoreType.DMA((2, 4)), pltpu.SemaphoreType.DMA((2, 4)),
    ]
    pdk, pdv, rdk, rdv, ff = pl.pallas_call(
        kernel,
        out_shape=[
            jax.ShapeDtypeStruct((64, 512), BF), jax.ShapeDtypeStruct((64, 512), BF),
            jax.ShapeDtypeStruct((128, 512), BF), jax.ShapeDtypeStruct((128, 512), BF),
            jax.ShapeDtypeStruct((2, 4, 4, 16, PW), BF),
        ],
        in_specs=[vmem] * 11,
        out_specs=[vmem] * 5,
        scratch_shapes=scratch,
        compiler_params=pltpu.CompilerParams(
            collective_id=0, has_side_effects=True, vmem_limit_bytes=60 << 20
        ),
    )(
        hidden, queries, answer_token_keys, answer_token_values, cotangent,
        slot_answer_index.reshape(1, SLOTS), rewards, group_prompt_keys, group_prompt_values,
        adapter_down_matrix, adapter_up_matrix,
    )
    pieces = ff.reshape(2, 4, 2, 2, 16, PW)
    grad_a = pieces[..., :AW].transpose(1, 3, 5, 0, 2, 4).reshape(WIDTH, RANK).astype(F32)
    grad_up = pieces[..., AW:].transpose(0, 2, 4, 1, 3, 5).reshape(RANK, FEATURES).astype(F32)
    return pdk, pdv, rdk, rdv, grad_a, grad_up


def solution(mesh):
    rows = P(("grp", "resp"), None)
    in_specs = (
        rows, rows, rows, rows, rows, P(("grp", "resp")), P("grp", None), rows, rows, P(), P(),
    )
    out_specs = (rows, rows, rows, rows, P(), P())
    return jax.shard_map(body, mesh=mesh, in_specs=in_specs, out_specs=out_specs, check_vma=False)
```

```python
import jax
import jax.numpy as jnp
from jax import lax
from jax.experimental import pallas as pl
from jax.experimental.pallas import tpu as pltpu
from jax.sharding import PartitionSpec as P

BF = jnp.bfloat16
F32 = jnp.float32
SLOTS = 128
D = 128
KVH = 4
QH = 8
SPAN = QH * D
PROMPT = 2048
RANK = 64
WIDTH = 5120
FEATURES = 4096
AW = WIDTH // KVH // 2
UW = SPAN // 2
PW = AW + UW
HW = WIDTH // KVH
FACTOR = D**-0.5
LOG2E_FACTOR = FACTOR * 1.4426950408889634
NN = (((1,), (0,)), ((), ()))
NT = (((1,), (1,)), ((), ()))


def mm(a, b, dims=NN):
    return lax.dot_general(a, b, dims, preferred_element_type=F32)


def fold(x, op):
    rows, lanes = x.shape
    return op(x.reshape(rows // 8, 8, lanes), axis=0)


def lanes(start, size):
    return pl.ds(pl.multiple_of(start, 128), size)


def kernel(
    hidden, queries, ans_k, ans_v, cot, slots, rewards, prompt_k, prompt_v, down_t, up,
    grads_out, ff_out,
    hid, down_v, up_v, cot_v, pk, pv, zb, kv, qb, gb, hb, rkv, masks, lows, gfull,
    s_ref, dp_ref, ds_ref, kt, dkv, bl, rd_send, rd, up_acc, blt,
    sb, yb, zr, pf, pr, ysum,
    g_own, g_send, g_recv, z_all, ff,
    send_sem, recv_sem, blk_send, blk_recv, bl_send, bl_recv, rd_send_sem, rd_recv_sem, local_sem,
):
    g = lax.axis_index("grp")
    r = lax.axis_index("resp")
    zl, core = lax.div(g, 2), lax.rem(g, 2)
    x, y, z = lax.div(r, 8), lax.rem(lax.div(r, 2), 4), lax.rem(r, 2)
    mesh_id = pl.DeviceIdType.MESH

    def at(gg, xx, yy, zz):
        return (gg, xx * 8 + yy * 2 + zz)

    xs = [lax.rem(x + d, 4) for d in range(4)]
    xf = [lax.rem(x + 4 - d, 4) for d in range(4)]
    ys = [lax.rem(y + d, 4) for d in range(4)]
    yf = [lax.rem(y + 4 - d, 4) for d in range(4)]
    x_dev = [at(g, xs[d], y, z) for d in range(4)]
    y_dev = [at(g, x, ys[d], z) for d in range(4)]
    z_dev = at(g, x, y, 1 - z)
    other_g = zl * 2 + 1 - core
    c_dev = at(other_g, x, y, z)
    ring = []
    for dz in range(4):
        for e in range(2):
            if dz or e:
                zz = z if e == 0 else 1 - z
                ring.append((dz, e, lax.rem(zl + dz, 4), lax.rem(zl + 4 - dz, 4), zz))
    column = []
    for dc in range(2):
        for dy in range(4):
            if dc or dy:
                column.append((dc, dy, core if dc == 0 else 1 - core, g if dc == 0 else other_g))
    plane = []
    for dx in (0, 1, 3, 2):
        for dy in (0, 1, 3, 2):
            if dx or dy:
                plane.append((dx, dy))

    def fetch(n, src, dst):
        c = pltpu.make_async_copy(src, dst, local_sem.at[n])
        c.start()
        return c

    loads = [
        fetch(0, prompt_k.at[:, lanes(x * D, D)], pk),
        fetch(1, prompt_v.at[:, lanes(x * D, D)], pv),
        fetch(2, cot, cot_v),
        fetch(3, hidden, hid),
        fetch(4, down_t, down_v),
        fetch(5, queries.at[:, lanes(x * SPAN, SPAN)], qb.at[x]),
        fetch(6, ans_k.at[:, lanes(x * D, D)], rkv.at[x, 0]),
        fetch(7, ans_v.at[:, lanes(x * D, D)], rkv.at[x, 1]),
        fetch(8, up.at[:, lanes(x * SPAN, SPAN)], up_v),
        fetch(9, hidden.at[:, lanes(x * HW, HW)], hb.at[x]),
    ]

    barrier = pltpu.get_barrier_semaphore()
    peers = [at(to * 2 + core, x, y, zz) for dz, e, to, frm, zz in ring]
    peers += [at(gg, x, ys[dy], z) for dc, dy, cc, gg in column]
    peers += [at(g, xs[dx], ys[dy], z) for dx, dy in plane if dx]
    for peer in peers:
        pl.semaphore_signal(barrier, inc=1, device_id=peer, device_id_type=mesh_id)
    pl.semaphore_wait(barrier, len(peers))

    sent = []
    names = {}

    def copy(name, src, dst, dev):
        k = names.setdefault(name, len(names))
        return pltpu.make_async_remote_copy(
            src_ref=src, dst_ref=dst, send_sem=send_sem.at[k], recv_sem=recv_sem.at[k],
            device_id=dev, device_id_type=mesh_id,
        )

    def send(name, src, dst, dev):
        c = copy(name, src, dst, dev)
        c.start()
        sent.append(c)

    def recv(name, dst, dev):
        copy(name, dst, dst, dev).wait_recv()

    def half(zz):
        return pl.ds(pl.multiple_of(zz * 64, 64), 64)

    def x_send(part, n, source, zz):
        for d in (1, 3, 2):
            send(
                ("x", part, n, d), source.at[:, lanes(xs[d] * D, D)],
                kv.at[n, x, y, half(zz)], x_dev[d],
            )

    def x_recv(part, n, zz):
        for d in (1, 2, 3):
            recv(("x", part, n, d), kv.at[n, xf[d], y, half(zz)], x_dev[d])

    def y_send(part, n, zz):
        for d in (1, 2, 3):
            send(("y", part, n, d), kv.at[n, :, y, half(zz)], kv.at[n, :, y, half(zz)], y_dev[d])

    def y_recv(part, n, zz):
        for d in (1, 2, 3):
            recv(("y", part, n, d), kv.at[n, :, yf[d], half(zz)], y_dev[d])

    send(("z", 0), prompt_k, zb.at[0], z_dev)
    x_send(0, 0, prompt_k, z)
    send(("z", 1), prompt_v, zb.at[1], z_dev)
    x_send(0, 1, prompt_v, z)

    across = jnp.broadcast_to(slots[...].astype(F32), (SLOTS, SLOTS))
    down_rows = across.T
    first = lax.broadcasted_iota(jnp.int32, (SLOTS, SLOTS), 0)
    second = lax.broadcasted_iota(jnp.int32, (SLOTS, SLOTS), 1)
    same = across == down_rows
    seen = same & (down_rows >= 0.0) & (first <= second)
    masks[x] = jnp.where(seen, 1.0, 0.0).astype(BF)
    reward = rewards[...]
    centred = reward - jnp.mean(reward, axis=1, keepdims=True)
    advantage = centred / jnp.sqrt(jnp.mean(centred * centred, axis=1, keepdims=True) + 1e-5)
    counts = jnp.sum(jnp.where(same, 1.0, 0.0), axis=1, keepdims=True)
    holds = down_rows[:, :64] == second[:, :64].astype(F32)
    weight = jnp.sum(jnp.where(holds, advantage, 0.0), axis=1, keepdims=True)
    weight = weight / jnp.maximum(counts, 1.0)
    loads[0].wait()
    loads[1].wait()
    kv[0, x, y, half(z), :] = pk[...]
    kv[1, x, y, half(z), :] = pv[...]
    x_recv(0, 0, z)
    y_send(0, 0, z)
    loads[2].wait()
    for c in range(0, FEATURES, 512):
        gfull[:, c : c + 512] = (cot_v[:, c : c + 512].astype(F32) * weight).astype(BF)
    x_recv(0, 1, z)
    y_send(0, 1, z)
    recv(("z", 0), zb.at[0], z_dev)
    x_send(1, 0, zb.at[0], 1 - z)
    kv[0, x, y, half(1 - z), :] = zb[0, :, lanes(x * D, D)]
    x_recv(1, 0, 1 - z)
    y_send(1, 0, 1 - z)
    recv(("z", 1), zb.at[1], z_dev)
    x_send(1, 1, zb.at[1], 1 - z)
    kv[1, x, y, half(1 - z), :] = zb[1, :, lanes(x * D, D)]

    def block_copies(i, src, dev, to):
        pairs = (
            (queries.at[:, lanes(to * SPAN, SPAN)], qb.at[src]),
            (gfull.at[:, lanes(to * SPAN, SPAN)], gb.at[src]),
            (ans_k.at[:, lanes(to * D, D)], rkv.at[src, 0]),
            (ans_v.at[:, lanes(to * D, D)], rkv.at[src, 1]),
            (masks.at[x], masks.at[src]),
            (lows.at[x], lows.at[src]),
            (hidden.at[:, lanes(to * HW, HW)], hb.at[src]),
        )
        return [
            pltpu.make_async_remote_copy(
                src_ref=a, dst_ref=b, send_sem=blk_send.at[n, i], recv_sem=blk_recv.at[n, i],
                device_id=dev, device_id_type=mesh_id,
            )
            for n, (a, b) in enumerate(pairs)
        ]

    x_recv(1, 1, 1 - z)
    y_send(1, 1, 1 - z)
    steps = ((1, 1), (2, 3), (3, 2))
    def block_send(i, d, which):
        for c in block_copies(i, x, x_dev[d], xs[d])[which]:
            c.start()

    block_send(1, 1, slice(0, 5))
    block_send(2, 3, slice(0, 5))
    loads[3].wait()
    loads[4].wait()
    lows[x] = mm(down_v[...], hid[...], NT).astype(BF)
    for i, d in steps:
        block_send(i, d, slice(5, 6))

    gb[x] = gfull[:, lanes(x * SPAN, SPAN)]
    dkv[...] = jnp.zeros_like(dkv)
    up_acc[...] = jnp.zeros_like(up_acc)
    for n in range(5, 10):
        loads[n].wait()
    y_recv(0, 0, z)
    y_recv(1, 0, 1 - z)

    def rd_copy(i, src, dev):
        return pltpu.make_async_remote_copy(
            src_ref=rd_send.at[i], dst_ref=rd.at[src],
            send_sem=rd_send_sem.at[i], recv_sem=rd_recv_sem.at[i],
            device_id=dev, device_id_type=mesh_id,
        )

    def bl_copy(i, d, head, block):
        return pltpu.make_async_remote_copy(
            src_ref=bl.at[head, block], dst_ref=bl.at[head, block],
            send_sem=bl_send.at[d, i], recv_sem=bl_recv.at[d, i],
            device_id=x_dev[d], device_id_type=mesh_id,
        )

    def step_of(i):
        return lax.rem(lax.div(i * (i + 1), 2), 4)

    def block(i, carry):
        src = lax.rem(x + 4 - step_of(i), 4)

        @pl.when(i > 0)
        def _():
            for c in block_copies(i, src, at(g, src, y, z), x)[:5]:
                c.wait_recv()

        @pl.when(i == 1)
        def _():
            block_send(3, 2, slice(0, 5))

        @pl.when(i == 2)
        def _():
            for n, d in steps:
                block_send(n, d, slice(6, 7))

        kt[:, PROMPT:] = rkv[src, 0].T
        mask = masks[src]
        mask = jnp.concatenate([mask] * QH, axis=1) > 0
        q = jnp.concatenate([qb[src, :, j * D : (j + 1) * D] for j in range(QH)], axis=0)
        go = jnp.concatenate([gb[src, :, j * D : (j + 1) * D] for j in range(QH)], axis=0)

        def rows(n, c):
            return rkv[src, n] if c == 16 else kv[n, c // 4, c % 4]

        def span(c):
            return slice(c * D, (c + 1) * D)

        top = None
        for c in range(17):
            s = mm(rows(0, c), q, NT)
            if c == 16:
                s = jnp.where(mask, s, -1e30)
            s_ref[span(c), :] = s
            part = fold(s, jnp.max)
            top = part if top is None else jnp.maximum(top, part)
        top = jnp.max(top, axis=0, keepdims=True) * LOG2E_FACTOR
        total = None
        for c in range(17):
            e = jnp.exp2(s_ref[span(c), :] * LOG2E_FACTOR - top)
            s_ref[span(c), :] = e
            part = fold(e, jnp.sum)
            total = part if total is None else total + part
        inv = 1.0 / jnp.sum(total, axis=0, keepdims=True)

        @pl.when(i == 0)
        def _():
            for c in range(16):
                kt[:, c * D : (c + 1) * D] = kv[0, c // 4, c % 4].T
            y_recv(0, 1, z)
            y_recv(1, 1, 1 - z)

        delta = None
        for c in range(17):
            dp = mm(rows(1, c), go, NT)
            pb = (s_ref[span(c), :] * inv).astype(BF)
            dp_ref[span(c), :] = dp
            part = fold(pb.astype(F32) * dp, jnp.sum)
            delta = part if delta is None else delta + part
            gv = mm(pb, go)
            if c == 16:
                rd_send[i, 1] = gv.astype(BF)
            else:
                dkv[1, c // 4, c % 4] += gv
        delta = jnp.sum(delta, axis=0, keepdims=True)
        inv = inv * FACTOR

        @pl.when(i == 3)
        def _():
            sb[1] = dkv[1].astype(BF)
            for d in (1, 3, 2):
                copy(("gy", 1, d), sb.at[1, :, ys[d]], yb.at[1, d - 1], y_dev[d]).start()

        for c in range(17):
            ds = (s_ref[span(c), :] * inv * (dp_ref[span(c), :] - delta)).astype(BF)
            ds_ref[span(c), :] = ds
        dq = mm(kt[...], ds_ref[...]).astype(BF)
        back = jnp.zeros((RANK, SLOTS), F32)
        for j in range(QH):
            back += mm(up_v[:, j * D : (j + 1) * D], dq[:, j * D : (j + 1) * D])
        bl[x, src] = back
        for d in (1, 3, 2):
            bl_copy(i, d, x, src).start()

        @pl.when(i > 0)
        def _():
            block_copies(i, src, at(g, src, y, z), x)[5].wait_recv()

        for c in range(17):
            gk = mm(ds_ref[span(c), :], q)
            if c == 16:
                rd_send[i, 0] = gk.astype(BF)
            else:
                dkv[0, c // 4, c % 4] += gk
        low_t = lows[src]
        for j in range(QH):
            up_acc[:, j * D : (j + 1) * D] += mm(low_t, dq[:, j * D : (j + 1) * D], NT)

        @pl.when(i > 0)
        def _():
            rd_copy(i, x, at(g, src, y, z)).start()

        return carry

    lax.fori_loop(0, 4, block, 0)
    for d in (1, 3, 2):
        sent.append(copy(("gy", 1, d), sb.at[1, :, ys[d]], yb.at[1, d - 1], y_dev[d]))

    rd[x] = rd_send[0]
    sb[0] = dkv[0].astype(BF)
    for n in range(2):
        for h in range(2):
            for c in range(2):
                rows = slice(c * 32 + h * 16, c * 32 + h * 16 + 16)
                piece = 2.0 * up_acc[rows, n * UW : (n + 1) * UW]
                g_own[c, 2 * h + n, :, AW:PW] = piece
                g_send[c, 2 * h + n, :, AW:PW] = piece.astype(BF)

    for i, d in steps:
        block_copies(i, xf[d], x_dev[d], x)[6].wait_recv()
    for i, step in ((0, 0),) + steps:
        for d in (1, 3, 2):
            bl_copy(i, d, xf[d], lax.rem(xf[d] + 4 - step, 4)).wait_recv()
    for b in range(4):
        back = 2.0 * (bl[0, b] + bl[1, b] + bl[2, b] + bl[3, b])
        blt[:, b * SLOTS : (b + 1) * SLOTS] = back.astype(BF)
    for n in range(2):
        piece = mm(blt[...], hb[:, :, n * AW : (n + 1) * AW].reshape(4 * SLOTS, AW))
        for h in range(2):
            for c in range(2):
                rows = slice(c * 32 + h * 16, c * 32 + h * 16 + 16)
                g_own[c, 2 * h + n, :, 0:AW] = piece[rows]
                g_send[c, 2 * h + n, :, 0:AW] = piece[rows].astype(BF)
    for dc, dy, cc, gg in column:
        send(("ry", dc, dy), g_send.at[cc, ys[dy]], g_recv.at[dc * 4 + dy], at(gg, x, ys[dy], z))

    for d in (1, 3, 2):
        send(("gy", 0, d), sb.at[0, :, ys[d]], yb.at[0, d - 1], y_dev[d])

    def along_y(n):
        for d in (1, 2, 3):
            recv(("gy", n, d), yb.at[n, d - 1], y_dev[d])
        for xx in range(4):
            part = dkv[n, xx, y]
            for d in range(3):
                part += yb[n, d, xx].astype(F32)
            ysum[n, xx] = part
            sb[n, xx, y] = part.astype(BF)
        send(("gz", n), sb.at[n, :, y, half(1 - z)], zr.at[n], z_dev)

    def along_z(n):
        recv(("gz", n), zr.at[n], z_dev)
        for xx in range(4):
            part = ysum[n, xx, half(z), :] + zr[n, xx].astype(F32)
            pf[xx, n] = part.astype(BF)

    along_y(1)
    for dc, dy, cc, gg in column:
        recv(("ry", dc, dy), g_recv.at[dc * 4 + dy], at(gg, x, ys[dy], z))
    part = g_own[core, y]
    for dc, dy, cc, gg in column:
        part += g_recv[dc * 4 + dy].astype(F32)
    here = zl * 2 + z
    z_all[here] = part.astype(BF)
    for dz, e, to, frm, zz in ring:
        send(("rz", dz, e), z_all.at[here], z_all.at[here], at(to * 2 + core, x, y, zz))
    along_y(0)
    along_z(1)
    for dz, e, to, frm, zz in ring:
        recv(("rz", dz, e), z_all.at[frm * 2 + zz], at(to * 2 + core, x, y, zz))
    total = z_all[0].astype(F32)
    for n in range(1, 8):
        total += z_all[n].astype(F32)
    ff[core, x, y] = total.astype(BF)
    for dx, dy in plane:
        send(("fp", dx, dy), ff.at[core, x, y], ff.at[core, x, y], at(g, xs[dx], ys[dy], z))
    along_z(0)
    for d in (1, 3, 2):
        send(("gx", d), pf.at[xs[d]], pr.at[x], x_dev[d])
    pr[x] = pf[x]
    for i, d in steps:
        rd_copy(i, xf[d], x_dev[d]).wait_recv()
    for h in range(4):
        grads_out[128:256, h * D : (h + 1) * D] = rd[h, 0]
        grads_out[256:384, h * D : (h + 1) * D] = rd[h, 1]
    for dx in (0, 1, 3, 2):
        for dy in (0, 1, 3, 2):
            if dx or dy:
                recv(("fp", dx, dy), ff.at[core, xf[dx], yf[dy]], at(g, xs[dx], ys[dy], z))
        send(("fc", dx), ff.at[core, xf[dx]], ff.at[core, xf[dx]], c_dev)
    for d in (1, 2, 3):
        recv(("gx", d), pr.at[xf[d]], x_dev[d])
    for h in range(4):
        grads_out[0:64, h * D : (h + 1) * D] = pr[h, 0]
        grads_out[64:128, h * D : (h + 1) * D] = pr[h, 1]
    ff_out[core] = ff[core]
    for d in range(4):
        recv(("fc", d), ff.at[1 - core, xf[d]], c_dev)
    ff_out[1 - core] = ff[1 - core]

    for c in sent:
        c.wait_send()
    for i, d in steps:
        for c in block_copies(i, x, x_dev[d], xs[d]):
            c.wait_send()
    for i, step in ((0, 0),) + steps:
        for d in (1, 3, 2):
            bl_copy(i, d, x, x).wait_send()
    for i, d in steps:
        rd_copy(i, x, x_dev[0]).wait_send()


def finish(grads, ff, pdk, pdv, rdk, rdv, ga, gu, ff_v, ga_v, gu_v, sem):
    small = [
        pltpu.make_async_copy(grads.at[rows], dst, sem.at[n])
        for n, (rows, dst) in enumerate(
            ((slice(0, 64), pdk), (slice(64, 128), pdv), (slice(128, 256), rdk), (slice(256, 384), rdv))
        )
    ]
    loads = [
        pltpu.make_async_copy(ff.at[:, xx], ff_v.at[:, xx], sem.at[4 + xx]) for xx in range(4)
    ]
    for c in loads + small:
        c.start()
    stores = []
    for xx in range(4):
        loads[xx].wait()
        for c in range(2):
            for p in range(4):
                rows = slice(c * 32 + (p // 2) * 16, c * 32 + (p // 2) * 16 + 16)
                n = 2 * xx + p % 2
                ga_v[rows, n * AW : (n + 1) * AW] = ff_v[c, xx, p, :, 0:AW].astype(F32)
                gu_v[rows, n * UW : (n + 1) * UW] = ff_v[c, xx, p, :, AW:PW].astype(F32)
        for k, (src, dst, w) in enumerate(((ga_v, ga, 2 * AW), (gu_v, gu, 2 * UW))):
            cols = slice(xx * w, (xx + 1) * w)
            c = pltpu.make_async_copy(src.at[:, cols], dst.at[:, cols], sem.at[8 + 2 * xx + k])
            c.start()
            stores.append(c)
    for c in small + stores:
        c.wait()


def body(
    hidden, queries, answer_token_keys, answer_token_values, cotangent, slot_answer_index,
    rewards, group_prompt_keys, group_prompt_values, adapter_down_matrix, adapter_up_matrix,
):
    vmem = pl.BlockSpec(memory_space=pltpu.VMEM)
    hbm = pl.BlockSpec(memory_space=pl.ANY)
    v = pltpu.VMEM
    scratch = [
        v((SLOTS, WIDTH), BF), v((RANK, WIDTH), BF), v((RANK, SPAN), BF), v((SLOTS, FEATURES), BF),
        v((64, D), BF), v((64, D), BF),
        v((2, 64, 512), BF), v((2, 4, 4, 128, D), BF),
        v((4, SLOTS, SPAN), BF), v((4, SLOTS, SPAN), BF), v((4, SLOTS, HW), BF),
        v((4, 2, SLOTS, D), BF), v((4, SLOTS, SLOTS), BF), v((4, RANK, SLOTS), BF), v((SLOTS, FEATURES), BF),
        v((PROMPT + SLOTS, SPAN), F32), v((PROMPT + SLOTS, SPAN), F32),
        v((PROMPT + SLOTS, SPAN), BF), v((D, PROMPT + SLOTS), BF),
        v((2, 4, 4, 128, D), F32), v((4, 4, RANK, SLOTS), F32),
        v((4, 2, SLOTS, D), BF), v((4, 2, SLOTS, D), BF),
        v((RANK, SPAN), F32), v((RANK, 4 * SLOTS), BF),
        v((2, 4, 4, 128, D), BF), v((2, 3, 4, 128, D), BF),
        v((2, 4, 64, D), BF), v((4, 2, 64, D), BF), v((4, 2, 64, D), BF),
        v((2, 4, 128, D), F32),
        v((2, 4, 16, PW), F32), v((2, 4, 16, PW), BF), v((8, 16, PW), BF),
        v((8, 16, PW), BF), v((2, 4, 4, 16, PW), BF),
        pltpu.SemaphoreType.DMA((96,)), pltpu.SemaphoreType.DMA((96,)),
        pltpu.SemaphoreType.DMA((7, 4)), pltpu.SemaphoreType.DMA((7, 4)),
        pltpu.SemaphoreType.DMA((4, 4)), pltpu.SemaphoreType.DMA((4, 4)),
        pltpu.SemaphoreType.DMA((4,)), pltpu.SemaphoreType.DMA((4,)),
        pltpu.SemaphoreType.DMA((10,)),
    ]
    grads, ff = pl.pallas_call(
        kernel,
        out_shape=[
            jax.ShapeDtypeStruct((384, 512), BF),
            jax.ShapeDtypeStruct((2, 4, 4, 16, PW), BF),
        ],
        in_specs=[hbm] * 5 + [vmem] * 2 + [hbm] * 4,
        out_specs=[vmem] * 2,
        scratch_shapes=scratch,
        compiler_params=pltpu.CompilerParams(
            collective_id=0, has_side_effects=True, vmem_limit_bytes=60 << 20
        ),
    )(
        hidden, queries, answer_token_keys, answer_token_values, cotangent,
        slot_answer_index.reshape(1, SLOTS), rewards, group_prompt_keys, group_prompt_values,
        adapter_down_matrix.T, adapter_up_matrix,
    )
    pdk, pdv, rdk, rdv, ga, gu = pl.pallas_call(
        finish,
        out_shape=[
            jax.ShapeDtypeStruct((64, 512), BF), jax.ShapeDtypeStruct((64, 512), BF),
            jax.ShapeDtypeStruct((128, 512), BF), jax.ShapeDtypeStruct((128, 512), BF),
            jax.ShapeDtypeStruct((RANK, WIDTH), F32), jax.ShapeDtypeStruct((RANK, FEATURES), F32),
        ],
        in_specs=[hbm] * 2,
        out_specs=[hbm] * 6,
        scratch_shapes=[
            v((2, 4, 4, 16, PW), BF), v((RANK, WIDTH), F32), v((RANK, FEATURES), F32),
            pltpu.SemaphoreType.DMA((16,)),
        ],
        compiler_params=pltpu.CompilerParams(vmem_limit_bytes=60 << 20),
    )(grads, ff)
    return pdk, pdv, rdk, rdv, ga.T, gu


def solution(mesh):
    rows = P(("grp", "resp"), None)
    in_specs = (
        rows, rows, rows, rows, rows, P(("grp", "resp")), P("grp", None), rows, rows, P(), P(),
    )
    out_specs = (rows, rows, rows, rows, P(), P())
    return jax.shard_map(body, mesh=mesh, in_specs=in_specs, out_specs=out_specs, check_vma=False)
```

```python
import jax
import jax.numpy as jnp
from jax import lax
from jax.experimental import pallas as pl
from jax.experimental.pallas import tpu as pltpu
from jax.sharding import PartitionSpec as P

BF = jnp.bfloat16
F32 = jnp.float32
SLOTS = 128
D = 128
KVH = 4
QH = 8
SPAN = QH * D
PROMPT = 2048
RANK = 64
WIDTH = 5120
FEATURES = 4096
AW = WIDTH // KVH // 2
UW = SPAN // 2
PW = AW + UW
HW = WIDTH // KVH
FACTOR = D**-0.5
LOG2E_FACTOR = FACTOR * 1.4426950408889634
NN = (((1,), (0,)), ((), ()))
NT = (((1,), (1,)), ((), ()))


def mm(a, b, dims=NN):
    return lax.dot_general(a, b, dims, preferred_element_type=F32)


def fold(x, op):
    rows, lanes = x.shape
    return op(x.reshape(rows // 8, 8, lanes), axis=0)


def lanes(start, size):
    return pl.ds(pl.multiple_of(start, 128), size)


def kernel(
    hidden, queries, ans_k, ans_v, cot, slots, rewards, prompt_k, prompt_v, down_t, up,
    grads_out, ff_out,
    hid, down_v, up_v, cot_v, pk, pv, zb, kv, qb, gb, hb, rkv, masks, lows, gfull,
    s_ref, dp_ref, ds_ref, kt, dkv, bl, bl_out, rd_send, rd, up_acc, blt,
    sb, yb, zr, pf, pr, ysum,
    a_own, a_send, a_recv, u_own, u_send, u_recv, z_all, ff,
    send_sem, recv_sem, blk_send, blk_recv, bl_send, bl_recv, rd_send_sem, rd_recv_sem, local_sem,
):
    g = lax.axis_index("grp")
    r = lax.axis_index("resp")
    zl, core = lax.div(g, 2), lax.rem(g, 2)
    x, y, z = lax.div(r, 8), lax.rem(lax.div(r, 2), 4), lax.rem(r, 2)
    mesh_id = pl.DeviceIdType.MESH

    def at(gg, xx, yy, zz):
        return (gg, xx * 8 + yy * 2 + zz)

    xs = [lax.rem(x + d, 4) for d in range(4)]
    xf = [lax.rem(x + 4 - d, 4) for d in range(4)]
    ys = [lax.rem(y + d, 4) for d in range(4)]
    yf = [lax.rem(y + 4 - d, 4) for d in range(4)]
    x_dev = [at(g, xs[d], y, z) for d in range(4)]
    y_dev = [at(g, x, ys[d], z) for d in range(4)]
    z_dev = at(g, x, y, 1 - z)
    other_g = zl * 2 + 1 - core
    c_dev = at(other_g, x, y, z)
    ring = []
    for dz in range(4):
        for e in range(2):
            if dz or e:
                zz = z if e == 0 else 1 - z
                ring.append((dz, e, lax.rem(zl + dz, 4), lax.rem(zl + 4 - dz, 4), zz))
    both = [(dc, dd) for dc in range(2) for dd in (1, 3, 2, 0) if dc or dd]
    cores, groups = (core, 1 - core), (g, other_g)
    plane = []
    for dx in (0, 1, 3, 2):
        for dy in (0, 1, 3, 2):
            if dx or dy:
                plane.append((dx, dy))

    def fetch(n, src, dst):
        c = pltpu.make_async_copy(src, dst, local_sem.at[n])
        c.start()
        return c

    loads = [
        fetch(0, prompt_k.at[:, lanes(x * D, D)], pk),
        fetch(1, prompt_v.at[:, lanes(x * D, D)], pv),
        fetch(2, cot, cot_v),
        fetch(3, hidden, hid),
        fetch(4, down_t, down_v),
        fetch(5, queries.at[:, lanes(x * SPAN, SPAN)], qb.at[x]),
        fetch(6, ans_k.at[:, lanes(x * D, D)], rkv.at[x, 0]),
        fetch(7, ans_v.at[:, lanes(x * D, D)], rkv.at[x, 1]),
        fetch(8, up.at[:, lanes(x * SPAN, SPAN)], up_v),
        fetch(9, hidden.at[:, lanes(y * HW, HW)], hb.at[y]),
    ]

    barrier = pltpu.get_barrier_semaphore()
    peers = [at(to * 2 + core, x, y, zz) for dz, e, to, frm, zz in ring]
    peers += [at(groups[dc], x, ys[d], z) for dc, d in both]
    peers += [at(other_g, xs[d], y, z) for d in (1, 2, 3)]
    peers += [at(g, xs[dx], ys[dy], z) for dx, dy in plane if dx]
    for peer in peers:
        pl.semaphore_signal(barrier, inc=1, device_id=peer, device_id_type=mesh_id)
    pl.semaphore_wait(barrier, len(peers))

    sent = []
    names = {}

    def copy(name, src, dst, dev):
        k = names.setdefault(name, len(names))
        return pltpu.make_async_remote_copy(
            src_ref=src, dst_ref=dst, send_sem=send_sem.at[k], recv_sem=recv_sem.at[k],
            device_id=dev, device_id_type=mesh_id,
        )

    def send(name, src, dst, dev):
        c = copy(name, src, dst, dev)
        c.start()
        sent.append(c)

    def recv(name, dst, dev):
        copy(name, dst, dst, dev).wait_recv()

    def half(zz):
        return pl.ds(pl.multiple_of(zz * 64, 64), 64)

    def x_send(part, n, source, zz):
        for d in (1, 3, 2):
            send(
                ("x", part, n, d), source.at[:, lanes(xs[d] * D, D)],
                kv.at[n, x, y, half(zz)], x_dev[d],
            )

    def x_recv(part, n, zz):
        for d in (1, 2, 3):
            recv(("x", part, n, d), kv.at[n, xf[d], y, half(zz)], x_dev[d])

    def y_send(part, n, zz):
        for d in (1, 2, 3):
            send(("y", part, n, d), kv.at[n, :, y, half(zz)], kv.at[n, :, y, half(zz)], y_dev[d])

    def y_recv(part, n, zz):
        for d in (1, 2, 3):
            recv(("y", part, n, d), kv.at[n, :, yf[d], half(zz)], y_dev[d])

    send(("z", 0), prompt_k, zb.at[0], z_dev)
    x_send(0, 0, prompt_k, z)
    send(("z", 1), prompt_v, zb.at[1], z_dev)
    x_send(0, 1, prompt_v, z)

    across = jnp.broadcast_to(slots[...].astype(F32), (SLOTS, SLOTS))
    down_rows = across.T
    first = lax.broadcasted_iota(jnp.int32, (SLOTS, SLOTS), 0)
    second = lax.broadcasted_iota(jnp.int32, (SLOTS, SLOTS), 1)
    same = across == down_rows
    seen = same & (down_rows >= 0.0) & (first <= second)
    masks[x] = jnp.where(seen, 1.0, 0.0).astype(BF)
    reward = rewards[...]
    centred = reward - jnp.mean(reward, axis=1, keepdims=True)
    advantage = centred / jnp.sqrt(jnp.mean(centred * centred, axis=1, keepdims=True) + 1e-5)
    counts = jnp.sum(jnp.where(same, 1.0, 0.0), axis=1, keepdims=True)
    holds = down_rows[:, :64] == second[:, :64].astype(F32)
    weight = jnp.sum(jnp.where(holds, advantage, 0.0), axis=1, keepdims=True)
    weight = weight / jnp.maximum(counts, 1.0)
    loads[0].wait()
    loads[1].wait()
    kv[0, x, y, half(z), :] = pk[...]
    kv[1, x, y, half(z), :] = pv[...]
    x_recv(0, 0, z)
    y_send(0, 0, z)
    loads[2].wait()
    for c in range(0, FEATURES, 512):
        gfull[:, c : c + 512] = (cot_v[:, c : c + 512].astype(F32) * weight).astype(BF)

    def block_copies(i, src, dev, to):
        pairs = (
            (queries.at[:, lanes(to * SPAN, SPAN)], qb.at[src]),
            (gfull.at[:, lanes(to * SPAN, SPAN)], gb.at[src]),
            (ans_k.at[:, lanes(to * D, D)], rkv.at[src, 0]),
            (ans_v.at[:, lanes(to * D, D)], rkv.at[src, 1]),
            (masks.at[x], masks.at[src]),
            (lows.at[x], lows.at[src]),
        )
        return [
            pltpu.make_async_remote_copy(
                src_ref=a, dst_ref=b, send_sem=blk_send.at[n, i], recv_sem=blk_recv.at[n, i],
                device_id=dev, device_id_type=mesh_id,
            )
            for n, (a, b) in enumerate(pairs)
        ]

    def block_send(i, d, which):
        for c in block_copies(i, x, x_dev[d], xs[d])[which]:
            c.start()

    block_send(1, 1, slice(0, 5))
    block_send(2, 3, slice(0, 5))
    x_recv(0, 1, z)
    y_send(0, 1, z)
    recv(("z", 0), zb.at[0], z_dev)
    x_send(1, 0, zb.at[0], 1 - z)
    kv[0, x, y, half(1 - z), :] = zb[0, :, lanes(x * D, D)]
    x_recv(1, 0, 1 - z)
    y_send(1, 0, 1 - z)
    recv(("z", 1), zb.at[1], z_dev)
    x_send(1, 1, zb.at[1], 1 - z)
    kv[1, x, y, half(1 - z), :] = zb[1, :, lanes(x * D, D)]

    x_recv(1, 1, 1 - z)
    y_send(1, 1, 1 - z)
    steps = ((1, 1), (2, 3), (3, 2))
    loads[3].wait()
    loads[4].wait()
    lows[x] = mm(down_v[...], hid[...], NT).astype(BF)
    for i, d in steps:
        block_send(i, d, slice(5, 6))

    gb[x] = gfull[:, lanes(x * SPAN, SPAN)]
    dkv[...] = jnp.zeros_like(dkv)
    up_acc[...] = jnp.zeros_like(up_acc)
    for n in range(5, 10):
        loads[n].wait()
    y_recv(0, 0, z)
    y_recv(1, 0, 1 - z)

    def rd_copy(i, src, dev):
        return pltpu.make_async_remote_copy(
            src_ref=rd_send.at[i], dst_ref=rd.at[src],
            send_sem=rd_send_sem.at[i], recv_sem=rd_recv_sem.at[i],
            device_id=dev, device_id_type=mesh_id,
        )

    def bl_copy(i, d, src):
        return pltpu.make_async_remote_copy(
            src_ref=bl_out.at[i], dst_ref=bl.at[x, y],
            send_sem=bl_send.at[d, i], recv_sem=bl_recv.at[d, i],
            device_id=at(g, src, ys[d], z), device_id_type=mesh_id,
        )

    def hid_copy(d):
        return copy(("hy", d), hidden.at[:, lanes(ys[d] * HW, HW)], hb.at[y], y_dev[d])

    def step_of(i):
        return lax.rem(lax.div(i * (i + 1), 2), 4)

    def block(i, carry):
        src = lax.rem(x + 4 - step_of(i), 4)

        @pl.when(i > 0)
        def _():
            for c in block_copies(i, src, at(g, src, y, z), x)[:5]:
                c.wait_recv()

        @pl.when(i == 1)
        def _():
            block_send(3, 2, slice(0, 5))
            for d in (1, 3, 2):
                hid_copy(d).start()

        kt[:, PROMPT:] = rkv[src, 0].T
        mask = masks[src]
        mask = jnp.concatenate([mask] * QH, axis=1) > 0
        q = jnp.concatenate([qb[src, :, j * D : (j + 1) * D] for j in range(QH)], axis=0)
        go = jnp.concatenate([gb[src, :, j * D : (j + 1) * D] for j in range(QH)], axis=0)

        def rows(n, c):
            if c == 8:
                return rkv[src, n]
            return kv[n, c // 2, (c % 2) * 2 : (c % 2) * 2 + 2].reshape(2 * D, D)

        def span(c):
            return slice(c * 2 * D, min((c + 1) * 2 * D, PROMPT + SLOTS))

        def gather_rows(n, c, value):
            if c == 8:
                rd_send[i, n] = value.astype(BF)
            else:
                dkv[n, c // 2, (c % 2) * 2 : (c % 2) * 2 + 2] += value.reshape(2, D, D)

        top = None
        for c in range(9):
            s = mm(rows(0, c), q, NT)
            if c == 8:
                s = jnp.where(mask, s, -1e30)
            s_ref[span(c), :] = s
            part = fold(s, jnp.max)
            top = part if top is None else jnp.maximum(top, part)
        top = jnp.max(top, axis=0, keepdims=True) * LOG2E_FACTOR
        total = None
        for c in range(9):
            e = jnp.exp2(s_ref[span(c), :] * LOG2E_FACTOR - top)
            s_ref[span(c), :] = e
            part = fold(e, jnp.sum)
            total = part if total is None else total + part
        inv = 1.0 / jnp.sum(total, axis=0, keepdims=True)

        @pl.when(i == 0)
        def _():
            for c in range(16):
                kt[:, c * D : (c + 1) * D] = kv[0, c // 4, c % 4].T
            y_recv(0, 1, z)
            y_recv(1, 1, 1 - z)

        delta = None
        for c in range(9):
            dp = mm(rows(1, c), go, NT)
            pb = (s_ref[span(c), :] * inv).astype(BF)
            dp_ref[span(c), :] = dp
            part = fold(pb.astype(F32) * dp, jnp.sum)
            delta = part if delta is None else delta + part
            gather_rows(1, c, mm(pb, go))
        delta = jnp.sum(delta, axis=0, keepdims=True)
        inv = inv * FACTOR

        @pl.when(i == 3)
        def _():
            sb[1] = dkv[1].astype(BF)
            for d in (1, 3, 2):
                copy(("gy", 1, d), sb.at[1, :, ys[d]], yb.at[1, d - 1], y_dev[d]).start()

        for c in range(9):
            ds = (s_ref[span(c), :] * inv * (dp_ref[span(c), :] - delta)).astype(BF)
            ds_ref[span(c), :] = ds
            gather_rows(0, c, mm(ds, q))
        dq = mm(kt[...], ds_ref[...]).astype(BF)
        back = jnp.zeros((RANK, SLOTS), F32)
        for j in range(QH):
            back += mm(up_v[:, j * D : (j + 1) * D], dq[:, j * D : (j + 1) * D])
        bl_out[i] = back
        for d in (1, 3, 2):
            bl_copy(i, d, src).start()

        @pl.when(i > 0)
        def _():
            bl_copy(i, 0, src).start()

        @pl.when(i > 0)
        def _():
            block_copies(i, src, at(g, src, y, z), x)[5].wait_recv()

        low_t = lows[src]
        for j in range(QH):
            up_acc[:, j * D : (j + 1) * D] += mm(low_t, dq[:, j * D : (j + 1) * D], NT)

        @pl.when(i > 0)
        def _():
            rd_copy(i, x, at(g, src, y, z)).start()

        return carry

    lax.fori_loop(0, 4, block, 0)
    for d in (1, 3, 2):
        sent.append(copy(("gy", 1, d), sb.at[1, :, ys[d]], yb.at[1, d - 1], y_dev[d]))

    for d in (1, 3, 2):
        sent.append(hid_copy(d))
    bl[x, y] = bl_out[0]
    rd[x] = rd_send[0]
    def pieces(own, out, n, value):
        for h in range(2):
            for c in range(2):
                part = value[c * 32 + h * 16 : c * 32 + h * 16 + 16]
                own[c, 2 * h + n] = part
                out[c, 2 * h + n] = part.astype(BF)

    for n in range(2):
        pieces(u_own, u_send, n, 2.0 * up_acc[:, n * UW : (n + 1) * UW])
    for dc, d in both:
        to = at(groups[dc], x, ys[d], z)
        send(("ru", dc, d), u_send.at[cores[dc], ys[d]], u_recv.at[dc * 4 + d], to)
    sb[0] = dkv[0].astype(BF)

    for d in (1, 2, 3):
        recv(("hy", d), hb.at[yf[d]], y_dev[d])
    for i, step in ((0, 0),) + steps:
        for d in (1, 3, 2, 0):
            if i or d:
                pltpu.make_async_remote_copy(
                    src_ref=bl_out.at[i], dst_ref=bl.at[xs[step], yf[d]],
                    send_sem=bl_send.at[d, i], recv_sem=bl_recv.at[d, i],
                    device_id=at(g, xs[step], yf[d], z), device_id_type=mesh_id,
                ).wait_recv()
    for b in range(4):
        back = 2.0 * (bl[0, b] + bl[1, b] + bl[2, b] + bl[3, b])
        blt[:, b * SLOTS : (b + 1) * SLOTS] = back.astype(BF)
    for n in range(2):
        part = mm(blt[...], hb[:, :, n * AW : (n + 1) * AW].reshape(4 * SLOTS, AW))
        pieces(a_own, a_send, n, part)
    for dc, d in both:
        to = at(groups[dc], xs[d], y, z)
        send(("ra", dc, d), a_send.at[cores[dc], xs[d]], a_recv.at[dc * 4 + d], to)
    part_u = u_own[core, y]
    for dc, d in both:
        recv(("ru", dc, d), u_recv.at[dc * 4 + d], at(groups[dc], x, ys[d], z))
        part_u += u_recv[dc * 4 + d].astype(F32)
    part_a = a_own[core, x]
    for dc, d in both:
        recv(("ra", dc, d), a_recv.at[dc * 4 + d], at(groups[dc], xs[d], y, z))
        part_a += a_recv[dc * 4 + d].astype(F32)
    here = zl * 2 + z
    z_all[here, :, 0:AW] = part_a.astype(BF)
    z_all[here, :, AW:PW] = part_u.astype(BF)
    for dz, e, to, frm, zz in ring:
        send(("rz", dz, e), z_all.at[here], z_all.at[here], at(to * 2 + core, x, y, zz))

    for d in (1, 3, 2):
        send(("gy", 0, d), sb.at[0, :, ys[d]], yb.at[0, d - 1], y_dev[d])
    for n in (1, 0):
        for d in (1, 2, 3):
            recv(("gy", n, d), yb.at[n, d - 1], y_dev[d])
        for xx in range(4):
            part = dkv[n, xx, y]
            for d in range(3):
                part += yb[n, d, xx].astype(F32)
            ysum[n, xx] = part
            sb[n, xx, y] = part.astype(BF)
    for i, d in steps:
        rd_copy(i, xf[d], x_dev[d]).wait_recv()
    for h in range(4):
        grads_out[128:256, h * D : (h + 1) * D] = rd[h, 0]
        grads_out[256:384, h * D : (h + 1) * D] = rd[h, 1]
    for dz, e, to, frm, zz in ring:
        recv(("rz", dz, e), z_all.at[frm * 2 + zz], at(to * 2 + core, x, y, zz))
    total = z_all[0].astype(F32)
    for n in range(1, 8):
        total += z_all[n].astype(F32)
    ff[core, x, y] = total.astype(BF)
    for dx, dy in plane:
        send(("fp", dx, dy), ff.at[core, x, y], ff.at[core, x, y], at(g, xs[dx], ys[dy], z))
    for n in range(2):
        send(("gz", n), sb.at[n, :, y, half(1 - z)], zr.at[n], z_dev)
    for n in range(2):
        recv(("gz", n), zr.at[n], z_dev)
        for xx in range(4):
            part = ysum[n, xx, half(z), :] + zr[n, xx].astype(F32)
            pf[xx, n] = part.astype(BF)
    for d in (1, 3, 2):
        send(("gx", d), pf.at[xs[d]], pr.at[x], x_dev[d])
    pr[x] = pf[x]
    for dx in (0, 1, 3, 2):
        for dy in (0, 1, 3, 2):
            if dx or dy:
                recv(("fp", dx, dy), ff.at[core, xf[dx], yf[dy]], at(g, xs[dx], ys[dy], z))
        send(("fc", dx), ff.at[core, xf[dx]], ff.at[core, xf[dx]], c_dev)
    for d in (1, 2, 3):
        recv(("gx", d), pr.at[xf[d]], x_dev[d])
    for h in range(4):
        grads_out[0:64, h * D : (h + 1) * D] = pr[h, 0]
        grads_out[64:128, h * D : (h + 1) * D] = pr[h, 1]
    ff_out[core] = ff[core]
    for d in range(4):
        recv(("fc", d), ff.at[1 - core, xf[d]], c_dev)
    ff_out[1 - core] = ff[1 - core]

    for c in sent:
        c.wait_send()
    for i, d in steps:
        for c in block_copies(i, x, x_dev[d], xs[d]):
            c.wait_send()
    for i, step in ((0, 0),) + steps:
        for d in (1, 3, 2):
            bl_copy(i, d, x).wait_send()
        if i:
            bl_copy(i, 0, x).wait_send()
    for i, d in steps:
        rd_copy(i, x, x_dev[0]).wait_send()


def finish(grads, ff, pdk, pdv, rdk, rdv, ga, gu, ff_v, ga_v, gu_v, sem):
    loads = [
        pltpu.make_async_copy(ff.at[:, xx], ff_v.at[:, xx], sem.at[xx]) for xx in range(4)
    ]
    for c in loads:
        c.start()
    pdk[...] = grads[0:64]
    pdv[...] = grads[64:128]
    rdk[...] = grads[128:256]
    rdv[...] = grads[256:384]
    stores = []
    for xx in range(4):
        loads[xx].wait()
        for c in range(2):
            top = c * 32 + (xx // 2) * 16
            for p in range(4):
                rows = slice(c * 32 + (p // 2) * 16, c * 32 + (p // 2) * 16 + 16)
                m, n = 2 * p + xx % 2, 2 * xx + p % 2
                ga_v[top : top + 16, m * AW : (m + 1) * AW] = ff_v[c, xx, p, :, 0:AW].astype(F32)
                gu_v[rows, n * UW : (n + 1) * UW] = ff_v[c, xx, p, :, AW:PW].astype(F32)
        cols = slice(2 * xx * UW, 2 * (xx + 1) * UW)
        done = [(gu_v.at[:, cols], gu.at[:, cols])]
        if xx % 2:
            for c in range(2):
                rows = slice(c * 32 + (xx // 2) * 16, c * 32 + (xx // 2) * 16 + 16)
                done.append((ga_v.at[rows], ga.at[rows]))
        for src, dst in done:
            stores.append(pltpu.make_async_copy(src, dst, sem.at[4 + len(stores)]))
            stores[-1].start()
    for c in stores:
        c.wait()


def body(
    hidden, queries, answer_token_keys, answer_token_values, cotangent, slot_answer_index,
    rewards, group_prompt_keys, group_prompt_values, adapter_down_matrix, adapter_up_matrix,
):
    vmem = pl.BlockSpec(memory_space=pltpu.VMEM)
    hbm = pl.BlockSpec(memory_space=pl.ANY)
    v = pltpu.VMEM
    scratch = [
        v((SLOTS, WIDTH), BF), v((RANK, WIDTH), BF), v((RANK, SPAN), BF), v((SLOTS, FEATURES), BF),
        v((64, D), BF), v((64, D), BF),
        v((2, 64, 512), BF), v((2, 4, 4, 128, D), BF),
        v((4, SLOTS, SPAN), BF), v((4, SLOTS, SPAN), BF), v((4, SLOTS, HW), BF),
        v((4, 2, SLOTS, D), BF), v((4, SLOTS, SLOTS), BF), v((4, RANK, SLOTS), BF), v((SLOTS, FEATURES), BF),
        v((PROMPT + SLOTS, SPAN), F32), v((PROMPT + SLOTS, SPAN), F32),
        v((PROMPT + SLOTS, SPAN), BF), v((D, PROMPT + SLOTS), BF),
        v((2, 4, 4, 128, D), F32), v((4, 4, RANK, SLOTS), F32), v((4, RANK, SLOTS), F32),
        v((4, 2, SLOTS, D), BF), v((4, 2, SLOTS, D), BF),
        v((RANK, SPAN), F32), v((RANK, 4 * SLOTS), BF),
        v((2, 4, 4, 128, D), BF), v((2, 3, 4, 128, D), BF),
        v((2, 4, 64, D), BF), v((4, 2, 64, D), BF), v((4, 2, 64, D), BF),
        v((2, 4, 128, D), F32),
        v((2, 4, 16, AW), F32), v((2, 4, 16, AW), BF), v((8, 16, AW), BF),
        v((2, 4, 16, UW), F32), v((2, 4, 16, UW), BF), v((8, 16, UW), BF),
        v((8, 16, PW), BF), v((2, 4, 4, 16, PW), BF),
        pltpu.SemaphoreType.DMA((96,)), pltpu.SemaphoreType.DMA((96,)),
        pltpu.SemaphoreType.DMA((6, 4)), pltpu.SemaphoreType.DMA((6, 4)),
        pltpu.SemaphoreType.DMA((4, 4)), pltpu.SemaphoreType.DMA((4, 4)),
        pltpu.SemaphoreType.DMA((4,)), pltpu.SemaphoreType.DMA((4,)),
        pltpu.SemaphoreType.DMA((10,)),
    ]
    grads, ff = pl.pallas_call(
        kernel,
        out_shape=[
            jax.ShapeDtypeStruct((384, 512), BF),
            jax.ShapeDtypeStruct((2, 4, 4, 16, PW), BF),
        ],
        in_specs=[hbm] * 5 + [vmem] * 2 + [hbm] * 4,
        out_specs=[vmem] * 2,
        scratch_shapes=scratch,
        compiler_params=pltpu.CompilerParams(
            collective_id=0, has_side_effects=True, vmem_limit_bytes=60 << 20
        ),
    )(
        hidden, queries, answer_token_keys, answer_token_values, cotangent,
        slot_answer_index.reshape(1, SLOTS), rewards, group_prompt_keys, group_prompt_values,
        adapter_down_matrix.T, adapter_up_matrix,
    )
    pdk, pdv, rdk, rdv, ga, gu = pl.pallas_call(
        finish,
        out_shape=[
            jax.ShapeDtypeStruct((64, 512), BF), jax.ShapeDtypeStruct((64, 512), BF),
            jax.ShapeDtypeStruct((128, 512), BF), jax.ShapeDtypeStruct((128, 512), BF),
            jax.ShapeDtypeStruct((RANK, WIDTH), F32), jax.ShapeDtypeStruct((RANK, FEATURES), F32),
        ],
        in_specs=[vmem, hbm],
        out_specs=[vmem] * 4 + [hbm] * 2,
        scratch_shapes=[
            v((2, 4, 4, 16, PW), BF), v((RANK, WIDTH), F32), v((RANK, FEATURES), F32),
            pltpu.SemaphoreType.DMA((12,)),
        ],
        compiler_params=pltpu.CompilerParams(vmem_limit_bytes=60 << 20),
    )(grads, ff)
    return pdk, pdv, rdk, rdv, ga.T, gu


def solution(mesh):
    rows = P(("grp", "resp"), None)
    in_specs = (
        rows, rows, rows, rows, rows, P(("grp", "resp")), P("grp", None), rows, rows, P(), P(),
    )
    out_specs = (rows, rows, rows, rows, P(), P())
    return jax.shard_map(body, mesh=mesh, in_specs=in_specs, out_specs=out_specs, check_vma=False)
```

```python
import jax
import jax.numpy as jnp
from jax import lax
from jax.experimental import pallas as pl
from jax.experimental.pallas import tpu as pltpu
from jax.sharding import PartitionSpec as P

BF = jnp.bfloat16
F32 = jnp.float32
SLOTS = 128
D = 128
KVH = 4
QH = 8
SPAN = QH * D
PROMPT = 2048
RANK = 64
WIDTH = 5120
FEATURES = 4096
AW = WIDTH // KVH // 2
UW = SPAN // 2
PW = AW + UW
HW = WIDTH // KVH
FACTOR = D**-0.5
LOG2E_FACTOR = FACTOR * 1.4426950408889634
NN = (((1,), (0,)), ((), ()))
NT = (((1,), (1,)), ((), ()))


def mm(a, b, dims=NN):
    return lax.dot_general(a, b, dims, preferred_element_type=F32)


def fold(x, op):
    rows, lanes = x.shape
    return op(x.reshape(rows // 8, 8, lanes), axis=0)


def lanes(start, size):
    return pl.ds(pl.multiple_of(start, 128), size)


def kernel(
    hidden, queries, ans_k, ans_v, cot, slots, rewards, prompt_k, prompt_v, down_t, up,
    grads_out, ff_out,
    hid, down_v, up_v, cot_v, pk, pv, zb, kv, qb, gb, hb, rkv, masks, lows, gfull,
    s_ref, dp_ref, ds_ref, kt, dkv, bl, bl_out, rd_send, rd, up_acc, blt,
    sb, yb, zr, pf, pr, ysum,
    a_own, a_send, a_recv, u_own, u_send, u_recv, z_all, ff,
    send_sem, recv_sem, blk_send, blk_recv, bl_send, bl_recv, rd_send_sem, rd_recv_sem, local_sem,
):
    g = lax.axis_index("grp")
    r = lax.axis_index("resp")
    zl, core = lax.div(g, 2), lax.rem(g, 2)
    x, y, z = lax.div(r, 8), lax.rem(lax.div(r, 2), 4), lax.rem(r, 2)
    mesh_id = pl.DeviceIdType.MESH

    def at(gg, xx, yy, zz):
        return (gg, xx * 8 + yy * 2 + zz)

    xs = [lax.rem(x + d, 4) for d in range(4)]
    xf = [lax.rem(x + 4 - d, 4) for d in range(4)]
    ys = [lax.rem(y + d, 4) for d in range(4)]
    yf = [lax.rem(y + 4 - d, 4) for d in range(4)]
    x_dev = [at(g, xs[d], y, z) for d in range(4)]
    y_dev = [at(g, x, ys[d], z) for d in range(4)]
    z_dev = at(g, x, y, 1 - z)
    other_g = zl * 2 + 1 - core
    c_dev = at(other_g, x, y, z)
    ring = []
    for dz in range(4):
        for e in range(2):
            if dz or e:
                zz = z if e == 0 else 1 - z
                ring.append((dz, e, lax.rem(zl + dz, 4), lax.rem(zl + 4 - dz, 4), zz))
    both = [(dc, dd) for dc in range(2) for dd in (1, 3, 2, 0) if dc or dd]
    cores, groups = (core, 1 - core), (g, other_g)
    plane = []
    for dx in (0, 1, 3, 2):
        for dy in (0, 1, 3, 2):
            if dx or dy:
                plane.append((dx, dy))

    def fetch(n, src, dst):
        c = pltpu.make_async_copy(src, dst, local_sem.at[n])
        c.start()
        return c

    loads = [
        fetch(0, prompt_k.at[:, lanes(x * D, D)], pk),
        fetch(1, prompt_v.at[:, lanes(x * D, D)], pv),
        fetch(2, cot, cot_v),
        fetch(3, hidden, hid),
        fetch(4, down_t, down_v),
        fetch(5, queries.at[:, lanes(x * SPAN, SPAN)], qb.at[x]),
        fetch(6, ans_k.at[:, lanes(x * D, D)], rkv.at[x, 0]),
        fetch(7, ans_v.at[:, lanes(x * D, D)], rkv.at[x, 1]),
        fetch(8, up.at[:, lanes(x * SPAN, SPAN)], up_v),
        fetch(9, hidden.at[:, lanes(y * HW, HW)], hb.at[y]),
    ]

    barrier = pltpu.get_barrier_semaphore()
    peers = [at(to * 2 + core, x, y, zz) for dz, e, to, frm, zz in ring]
    peers += [at(groups[dc], x, ys[d], z) for dc, d in both]
    peers += [at(other_g, xs[d], y, z) for d in (1, 2, 3)]
    peers += [at(g, xs[dx], ys[dy], z) for dx, dy in plane if dx]
    for peer in peers:
        pl.semaphore_signal(barrier, inc=1, device_id=peer, device_id_type=mesh_id)
    pl.semaphore_wait(barrier, len(peers))

    sent = []
    names = {}

    def copy(name, src, dst, dev):
        k = names.setdefault(name, len(names))
        return pltpu.make_async_remote_copy(
            src_ref=src, dst_ref=dst, send_sem=send_sem.at[k], recv_sem=recv_sem.at[k],
            device_id=dev, device_id_type=mesh_id,
        )

    def send(name, src, dst, dev):
        c = copy(name, src, dst, dev)
        c.start()
        sent.append(c)

    def recv(name, dst, dev):
        copy(name, dst, dst, dev).wait_recv()

    def half(zz):
        return pl.ds(pl.multiple_of(zz * 64, 64), 64)

    def x_send(part, n, source, zz):
        for d in (1, 3, 2):
            send(
                ("x", part, n, d), source.at[:, lanes(xs[d] * D, D)],
                kv.at[n, x, y, half(zz)], x_dev[d],
            )

    def x_recv(part, n, zz):
        for d in (1, 2, 3):
            recv(("x", part, n, d), kv.at[n, xf[d], y, half(zz)], x_dev[d])

    def y_send(part, n, zz):
        for d in (1, 2, 3):
            send(("y", part, n, d), kv.at[n, :, y, half(zz)], kv.at[n, :, y, half(zz)], y_dev[d])

    def y_recv(part, n, zz):
        for d in (1, 2, 3):
            recv(("y", part, n, d), kv.at[n, :, yf[d], half(zz)], y_dev[d])

    send(("z", 0), prompt_k, zb.at[0], z_dev)
    x_send(0, 0, prompt_k, z)
    send(("z", 1), prompt_v, zb.at[1], z_dev)
    x_send(0, 1, prompt_v, z)

    across = jnp.broadcast_to(slots[...].astype(F32), (SLOTS, SLOTS))
    down_rows = across.T
    first = lax.broadcasted_iota(jnp.int32, (SLOTS, SLOTS), 0)
    second = lax.broadcasted_iota(jnp.int32, (SLOTS, SLOTS), 1)
    same = across == down_rows
    seen = same & (down_rows >= 0.0) & (first <= second)
    masks[x] = jnp.where(seen, 1.0, 0.0).astype(BF)
    reward = rewards[...]
    centred = reward - jnp.mean(reward, axis=1, keepdims=True)
    advantage = centred / jnp.sqrt(jnp.mean(centred * centred, axis=1, keepdims=True) + 1e-5)
    counts = jnp.sum(jnp.where(same, 1.0, 0.0), axis=1, keepdims=True)
    holds = down_rows[:, :64] == second[:, :64].astype(F32)
    weight = jnp.sum(jnp.where(holds, advantage, 0.0), axis=1, keepdims=True)
    weight = weight / jnp.maximum(counts, 1.0)
    loads[0].wait()
    loads[1].wait()
    kv[0, x, y, half(z), :] = pk[...]
    kv[1, x, y, half(z), :] = pv[...]
    x_recv(0, 0, z)
    y_send(0, 0, z)
    loads[2].wait()
    for c in range(0, FEATURES, 512):
        gfull[:, c : c + 512] = (cot_v[:, c : c + 512].astype(F32) * weight).astype(BF)

    def block_copies(i, src, dev, to):
        pairs = (
            (queries.at[:, lanes(to * SPAN, SPAN)], qb.at[src]),
            (gfull.at[:, lanes(to * SPAN, SPAN)], gb.at[src]),
            (ans_k.at[:, lanes(to * D, D)], rkv.at[src, 0]),
            (ans_v.at[:, lanes(to * D, D)], rkv.at[src, 1]),
            (masks.at[x], masks.at[src]),
            (lows.at[x], lows.at[src]),
        )
        return [
            pltpu.make_async_remote_copy(
                src_ref=a, dst_ref=b, send_sem=blk_send.at[n, i], recv_sem=blk_recv.at[n, i],
                device_id=dev, device_id_type=mesh_id,
            )
            for n, (a, b) in enumerate(pairs)
        ]

    def block_send(i, d, which):
        for c in block_copies(i, x, x_dev[d], xs[d])[which]:
            c.start()

    x_recv(0, 1, z)
    y_send(0, 1, z)
    recv(("z", 0), zb.at[0], z_dev)
    x_send(1, 0, zb.at[0], 1 - z)
    kv[0, x, y, half(1 - z), :] = zb[0, :, lanes(x * D, D)]
    x_recv(1, 0, 1 - z)
    y_send(1, 0, 1 - z)
    block_send(1, 1, slice(0, 5))
    block_send(2, 3, slice(0, 5))
    recv(("z", 1), zb.at[1], z_dev)
    x_send(1, 1, zb.at[1], 1 - z)
    kv[1, x, y, half(1 - z), :] = zb[1, :, lanes(x * D, D)]

    x_recv(1, 1, 1 - z)
    y_send(1, 1, 1 - z)
    steps = ((1, 1), (2, 3), (3, 2))
    loads[3].wait()
    loads[4].wait()
    lows[x] = mm(down_v[...], hid[...], NT).astype(BF)
    for i, d in steps:
        block_send(i, d, slice(5, 6))

    gb[x] = gfull[:, lanes(x * SPAN, SPAN)]
    dkv[...] = jnp.zeros_like(dkv)
    up_acc[...] = jnp.zeros_like(up_acc)
    for n in range(5, 10):
        loads[n].wait()
    y_recv(0, 0, z)
    y_recv(1, 0, 1 - z)

    def rd_copy(i, src, dev):
        return pltpu.make_async_remote_copy(
            src_ref=rd_send.at[i], dst_ref=rd.at[src],
            send_sem=rd_send_sem.at[i], recv_sem=rd_recv_sem.at[i],
            device_id=dev, device_id_type=mesh_id,
        )

    def bl_copy(i, d, src):
        return pltpu.make_async_remote_copy(
            src_ref=bl_out.at[i], dst_ref=bl.at[x, y],
            send_sem=bl_send.at[d, i], recv_sem=bl_recv.at[d, i],
            device_id=at(g, src, ys[d], z), device_id_type=mesh_id,
        )

    def hid_copy(d):
        return copy(("hy", d), hidden.at[:, lanes(ys[d] * HW, HW)], hb.at[y], y_dev[d])

    def step_of(i):
        return lax.rem(lax.div(i * (i + 1), 2), 4)

    def block(i, carry):
        src = lax.rem(x + 4 - step_of(i), 4)

        @pl.when(i > 0)
        def _():
            for c in block_copies(i, src, at(g, src, y, z), x)[:5]:
                c.wait_recv()

        @pl.when(i == 1)
        def _():
            block_send(3, 2, slice(0, 5))
            for d in (1, 3, 2):
                hid_copy(d).start()

        kt[:, PROMPT:] = rkv[src, 0].T
        mask = masks[src]
        mask = jnp.concatenate([mask] * QH, axis=1) > 0
        q = jnp.concatenate([qb[src, :, j * D : (j + 1) * D] for j in range(QH)], axis=0)
        go = jnp.concatenate([gb[src, :, j * D : (j + 1) * D] for j in range(QH)], axis=0)

        def rows(n, c):
            if c == 8:
                return rkv[src, n]
            return kv[n, c // 2, (c % 2) * 2 : (c % 2) * 2 + 2].reshape(2 * D, D)

        def span(c):
            return slice(c * 2 * D, min((c + 1) * 2 * D, PROMPT + SLOTS))

        def gather_rows(n, c, value):
            if c == 8:
                rd_send[i, n] = value.astype(BF)
            else:
                dkv[n, c // 2, (c % 2) * 2 : (c % 2) * 2 + 2] += value.reshape(2, D, D)

        top = None
        for c in range(9):
            s = mm(rows(0, c), q, NT)
            if c == 8:
                s = jnp.where(mask, s, -1e30)
            s_ref[span(c), :] = s
            part = fold(s, jnp.max)
            top = part if top is None else jnp.maximum(top, part)
        top = jnp.max(top, axis=0, keepdims=True) * LOG2E_FACTOR
        total = None
        for c in range(9):
            e = jnp.exp2(s_ref[span(c), :] * LOG2E_FACTOR - top)
            s_ref[span(c), :] = e
            part = fold(e, jnp.sum)
            total = part if total is None else total + part
        inv = 1.0 / jnp.sum(total, axis=0, keepdims=True)

        @pl.when(i == 0)
        def _():
            for c in range(16):
                kt[:, c * D : (c + 1) * D] = kv[0, c // 4, c % 4].T
            y_recv(0, 1, z)
            y_recv(1, 1, 1 - z)

        delta = None
        for c in range(9):
            dp = mm(rows(1, c), go, NT)
            pb = (s_ref[span(c), :] * inv).astype(BF)
            dp_ref[span(c), :] = dp
            part = fold(pb.astype(F32) * dp, jnp.sum)
            delta = part if delta is None else delta + part
            gather_rows(1, c, mm(pb, go))
        delta = jnp.sum(delta, axis=0, keepdims=True)
        inv = inv * FACTOR

        @pl.when(i == 3)
        def _():
            sb[1] = dkv[1].astype(BF)
            for d in (1, 3, 2):
                copy(("gy", 1, d), sb.at[1, :, ys[d]], yb.at[1, d - 1], y_dev[d]).start()

        for c in range(9):
            ds = (s_ref[span(c), :] * inv * (dp_ref[span(c), :] - delta)).astype(BF)
            ds_ref[span(c), :] = ds
            gather_rows(0, c, mm(ds, q))
        dq = mm(kt[...], ds_ref[...]).astype(BF)
        back = jnp.zeros((RANK, SLOTS), F32)
        for j in range(QH):
            back += mm(up_v[:, j * D : (j + 1) * D], dq[:, j * D : (j + 1) * D])
        bl_out[i] = back
        for d in (1, 3, 2):
            bl_copy(i, d, src).start()

        @pl.when(i > 0)
        def _():
            bl_copy(i, 0, src).start()

        @pl.when(i > 0)
        def _():
            block_copies(i, src, at(g, src, y, z), x)[5].wait_recv()

        low_t = lows[src]
        for j in range(QH):
            up_acc[:, j * D : (j + 1) * D] += mm(low_t, dq[:, j * D : (j + 1) * D], NT)

        @pl.when(i > 0)
        def _():
            rd_copy(i, x, at(g, src, y, z)).start()

        return carry

    lax.fori_loop(0, 4, block, 0)
    for d in (1, 3, 2):
        sent.append(copy(("gy", 1, d), sb.at[1, :, ys[d]], yb.at[1, d - 1], y_dev[d]))

    for d in (1, 3, 2):
        sent.append(hid_copy(d))
    bl[x, y] = bl_out[0]
    rd[x] = rd_send[0]
    def pieces(own, out, n, value):
        for h in range(2):
            for c in range(2):
                part = value[c * 32 + h * 16 : c * 32 + h * 16 + 16]
                own[c, 2 * h + n] = part
                out[c, 2 * h + n] = part.astype(BF)

    for n in range(2):
        pieces(u_own, u_send, n, 2.0 * up_acc[:, n * UW : (n + 1) * UW])
    for dc, d in both:
        to = at(groups[dc], x, ys[d], z)
        send(("ru", dc, d), u_send.at[cores[dc], ys[d]], u_recv.at[dc * 4 + d], to)
    sb[0] = dkv[0].astype(BF)

    for d in (1, 2, 3):
        recv(("hy", d), hb.at[yf[d]], y_dev[d])
    for i, step in ((0, 0),) + steps:
        for d in (1, 3, 2, 0):
            if i or d:
                pltpu.make_async_remote_copy(
                    src_ref=bl_out.at[i], dst_ref=bl.at[xs[step], yf[d]],
                    send_sem=bl_send.at[d, i], recv_sem=bl_recv.at[d, i],
                    device_id=at(g, xs[step], yf[d], z), device_id_type=mesh_id,
                ).wait_recv()
    for b in range(4):
        back = 2.0 * (bl[0, b] + bl[1, b] + bl[2, b] + bl[3, b])
        blt[:, b * SLOTS : (b + 1) * SLOTS] = back.astype(BF)
    for n in range(2):
        part = mm(blt[...], hb[:, :, n * AW : (n + 1) * AW].reshape(4 * SLOTS, AW))
        pieces(a_own, a_send, n, part)
    for dc, d in both:
        to = at(groups[dc], xs[d], y, z)
        send(("ra", dc, d), a_send.at[cores[dc], xs[d]], a_recv.at[dc * 4 + d], to)
    part_u = u_own[core, y]
    for dc, d in both:
        recv(("ru", dc, d), u_recv.at[dc * 4 + d], at(groups[dc], x, ys[d], z))
        part_u += u_recv[dc * 4 + d].astype(F32)
    part_a = a_own[core, x]
    for dc, d in both:
        recv(("ra", dc, d), a_recv.at[dc * 4 + d], at(groups[dc], xs[d], y, z))
        part_a += a_recv[dc * 4 + d].astype(F32)
    here = zl * 2 + z
    z_all[here, :, 0:AW] = part_a.astype(BF)
    z_all[here, :, AW:PW] = part_u.astype(BF)
    for dz, e, to, frm, zz in ring:
        send(("rz", dz, e), z_all.at[here], z_all.at[here], at(to * 2 + core, x, y, zz))

    for d in (1, 3, 2):
        send(("gy", 0, d), sb.at[0, :, ys[d]], yb.at[0, d - 1], y_dev[d])
    for n in (1, 0):
        for d in (1, 2, 3):
            recv(("gy", n, d), yb.at[n, d - 1], y_dev[d])
        for xx in range(4):
            part = dkv[n, xx, y]
            for d in range(3):
                part += yb[n, d, xx].astype(F32)
            ysum[n, xx] = part
            sb[n, xx, y] = part.astype(BF)
    for i, d in steps:
        rd_copy(i, xf[d], x_dev[d]).wait_recv()
    for h in range(4):
        grads_out[128:256, h * D : (h + 1) * D] = rd[h, 0]
        grads_out[256:384, h * D : (h + 1) * D] = rd[h, 1]
    for dz, e, to, frm, zz in ring:
        recv(("rz", dz, e), z_all.at[frm * 2 + zz], at(to * 2 + core, x, y, zz))
    total = z_all[0].astype(F32)
    for n in range(1, 8):
        total += z_all[n].astype(F32)
    ff[core, x, y] = total.astype(BF)
    for dx, dy in plane:
        send(("fp", dx, dy), ff.at[core, x, y], ff.at[core, x, y], at(g, xs[dx], ys[dy], z))
    for n in range(2):
        send(("gz", n), sb.at[n, :, y, half(1 - z)], zr.at[n], z_dev)
    for n in range(2):
        recv(("gz", n), zr.at[n], z_dev)
        for xx in range(4):
            part = ysum[n, xx, half(z), :] + zr[n, xx].astype(F32)
            pf[xx, n] = part.astype(BF)
    for d in (1, 3, 2):
        send(("gx", d), pf.at[xs[d]], pr.at[x], x_dev[d])
    pr[x] = pf[x]
    for dx in (0, 1, 3, 2):
        for dy in (0, 1, 3, 2):
            if dx or dy:
                recv(("fp", dx, dy), ff.at[core, xf[dx], yf[dy]], at(g, xs[dx], ys[dy], z))
        send(("fc", dx), ff.at[core, xf[dx]], ff.at[core, xf[dx]], c_dev)
    for d in (1, 2, 3):
        recv(("gx", d), pr.at[xf[d]], x_dev[d])
    for h in range(4):
        grads_out[0:64, h * D : (h + 1) * D] = pr[h, 0]
        grads_out[64:128, h * D : (h + 1) * D] = pr[h, 1]
    stores = [fetch(0, ff.at[core], ff_out.at[core])]
    for d in range(4):
        recv(("fc", d), ff.at[1 - core, xf[d]], c_dev)
        stores.append(fetch(1 + d, ff.at[1 - core, xf[d]], ff_out.at[1 - core, xf[d]]))
    for c in stores:
        c.wait()

    for c in sent:
        c.wait_send()
    for i, d in steps:
        for c in block_copies(i, x, x_dev[d], xs[d]):
            c.wait_send()
    for i, step in ((0, 0),) + steps:
        for d in (1, 3, 2):
            bl_copy(i, d, x).wait_send()
        if i:
            bl_copy(i, 0, x).wait_send()
    for i, d in steps:
        rd_copy(i, x, x_dev[0]).wait_send()


def finish(grads, ff, pdk, pdv, rdk, rdv, ga, gu, ff_v, ga_v, gu_v, sem):
    loads = [
        pltpu.make_async_copy(ff.at[:, xx], ff_v.at[:, xx], sem.at[xx]) for xx in range(4)
    ]
    for c in loads:
        c.start()
    pdk[...] = grads[0:64]
    pdv[...] = grads[64:128]
    rdk[...] = grads[128:256]
    rdv[...] = grads[256:384]
    stores = []
    for xx in range(4):
        loads[xx].wait()
        for c in range(2):
            top = c * 32 + (xx // 2) * 16
            for p in range(4):
                rows = slice(c * 32 + (p // 2) * 16, c * 32 + (p // 2) * 16 + 16)
                m, n = 2 * p + xx % 2, 2 * xx + p % 2
                ga_v[top : top + 16, m * AW : (m + 1) * AW] = ff_v[c, xx, p, :, 0:AW].astype(F32)
                gu_v[rows, n * UW : (n + 1) * UW] = ff_v[c, xx, p, :, AW:PW].astype(F32)
        cols = slice(2 * xx * UW, 2 * (xx + 1) * UW)
        done = [(gu_v.at[:, cols], gu.at[:, cols])]
        if xx % 2:
            for c in range(2):
                rows = slice(c * 32 + (xx // 2) * 16, c * 32 + (xx // 2) * 16 + 16)
                done.append((ga_v.at[rows], ga.at[rows]))
        for src, dst in done:
            stores.append(pltpu.make_async_copy(src, dst, sem.at[4 + len(stores)]))
            stores[-1].start()
    for c in stores:
        c.wait()


def body(
    hidden, queries, answer_token_keys, answer_token_values, cotangent, slot_answer_index,
    rewards, group_prompt_keys, group_prompt_values, adapter_down_matrix, adapter_up_matrix,
):
    vmem = pl.BlockSpec(memory_space=pltpu.VMEM)
    hbm = pl.BlockSpec(memory_space=pl.ANY)
    v = pltpu.VMEM
    scratch = [
        v((SLOTS, WIDTH), BF), v((RANK, WIDTH), BF), v((RANK, SPAN), BF), v((SLOTS, FEATURES), BF),
        v((64, D), BF), v((64, D), BF),
        v((2, 64, 512), BF), v((2, 4, 4, 128, D), BF),
        v((4, SLOTS, SPAN), BF), v((4, SLOTS, SPAN), BF), v((4, SLOTS, HW), BF),
        v((4, 2, SLOTS, D), BF), v((4, SLOTS, SLOTS), BF), v((4, RANK, SLOTS), BF), v((SLOTS, FEATURES), BF),
        v((PROMPT + SLOTS, SPAN), F32), v((PROMPT + SLOTS, SPAN), F32),
        v((PROMPT + SLOTS, SPAN), BF), v((D, PROMPT + SLOTS), BF),
        v((2, 4, 4, 128, D), F32), v((4, 4, RANK, SLOTS), F32), v((4, RANK, SLOTS), F32),
        v((4, 2, SLOTS, D), BF), v((4, 2, SLOTS, D), BF),
        v((RANK, SPAN), F32), v((RANK, 4 * SLOTS), BF),
        v((2, 4, 4, 128, D), BF), v((2, 3, 4, 128, D), BF),
        v((2, 4, 64, D), BF), v((4, 2, 64, D), BF), v((4, 2, 64, D), BF),
        v((2, 4, 128, D), F32),
        v((2, 4, 16, AW), F32), v((2, 4, 16, AW), BF), v((8, 16, AW), BF),
        v((2, 4, 16, UW), F32), v((2, 4, 16, UW), BF), v((8, 16, UW), BF),
        v((8, 16, PW), BF), v((2, 4, 4, 16, PW), BF),
        pltpu.SemaphoreType.DMA((96,)), pltpu.SemaphoreType.DMA((96,)),
        pltpu.SemaphoreType.DMA((6, 4)), pltpu.SemaphoreType.DMA((6, 4)),
        pltpu.SemaphoreType.DMA((4, 4)), pltpu.SemaphoreType.DMA((4, 4)),
        pltpu.SemaphoreType.DMA((4,)), pltpu.SemaphoreType.DMA((4,)),
        pltpu.SemaphoreType.DMA((10,)),
    ]
    grads, ff = pl.pallas_call(
        kernel,
        out_shape=[
            jax.ShapeDtypeStruct((384, 512), BF),
            jax.ShapeDtypeStruct((2, 4, 4, 16, PW), BF),
        ],
        in_specs=[hbm] * 5 + [vmem] * 2 + [hbm] * 4,
        out_specs=[vmem, hbm],
        scratch_shapes=scratch,
        compiler_params=pltpu.CompilerParams(
            collective_id=0, has_side_effects=True, vmem_limit_bytes=60 << 20
        ),
    )(
        hidden, queries, answer_token_keys, answer_token_values, cotangent,
        slot_answer_index.reshape(1, SLOTS), rewards, group_prompt_keys, group_prompt_values,
        adapter_down_matrix.T, adapter_up_matrix,
    )
    pdk, pdv, rdk, rdv, ga, gu = pl.pallas_call(
        finish,
        out_shape=[
            jax.ShapeDtypeStruct((64, 512), BF), jax.ShapeDtypeStruct((64, 512), BF),
            jax.ShapeDtypeStruct((128, 512), BF), jax.ShapeDtypeStruct((128, 512), BF),
            jax.ShapeDtypeStruct((RANK, WIDTH), F32), jax.ShapeDtypeStruct((RANK, FEATURES), F32),
        ],
        in_specs=[vmem, hbm],
        out_specs=[vmem] * 4 + [hbm] * 2,
        scratch_shapes=[
            v((2, 4, 4, 16, PW), BF), v((RANK, WIDTH), F32), v((RANK, FEATURES), F32),
            pltpu.SemaphoreType.DMA((12,)),
        ],
        compiler_params=pltpu.CompilerParams(vmem_limit_bytes=60 << 20),
    )(grads, ff)
    return pdk, pdv, rdk, rdv, ga.T, gu


def solution(mesh):
    rows = P(("grp", "resp"), None)
    in_specs = (
        rows, rows, rows, rows, rows, P(("grp", "resp")), P("grp", None), rows, rows, P(), P(),
    )
    out_specs = (rows, rows, rows, rows, P(), P())
    return jax.shard_map(body, mesh=mesh, in_specs=in_specs, out_specs=out_specs, check_vma=False)
```
